32 devices in a mesh: row: 4 (over y, x), col: 8 (over z, core).
Axes of the slice: x: 2, y: 2, z: 4, core: 2. Of those that a mesh axis runs over, the one named last changes fastest.
Arguments:
- inv_known: float32 [512, 512], P('row', 'col'), as said below
- pattern: int32 [8, 8], P('row', 'col'), may hold values from 0 to 1, as said below
- factor: float32 [512, 2, 512], P(('row', 'col')), may hold values from -0.25 to 0.25
- listed: int32 [512, 2], P(('row', 'col')), may hold values 0 or 1
- diag_inverse: float32 [512, 2, 512], P('col'), may hold values from -6 to 6
Outputs:
- inverse_columns: float32 [512, 2, 512], P('col', None, 'row')
- schur: float32 [512, 2, 512], P('col')
The draws below stay inside these ranges and needn't reach their ends.
Inputs may be any that keep to these rules, and one draw needn't show every extreme that they name: `inv_known`: symmetric. `pattern`: symmetric; every diagonal tile is present.
All inputs are finite; a program needn't handle non-finite values. No bound on the sum of `listed` on one device may be relied on, other than what follows from the above.
Results may differ from the reference program's by a relative error of at most 0.0001.
Values sent between devices are 32-bit elements; how exact they have to be, the bound alone decides.
No kernel may reach another device: no remote copies, remote signals or barrier semaphores. Data moves between devices by JAX's collectives and lax.ppermute only.
A program may use at most 64 MiB of HBM per device.

```python
import jax
import jax.numpy as jnp
from jax import lax

W = 512
KS = 2
TILE = 64
R = 512
RT = 8
N_COL = 8


def draw_inv_known(key, part):
    values = jax.random.normal(key, (R, R), jnp.float32)
    return (values + values.T) * 0.70710678


def draw_pattern(key, part):
    score = jax.random.randint(key, (RT, RT), 0, 5)
    upper = jnp.where(score < 3, 1, 0)
    index = jnp.arange(RT)
    mirrored = jnp.where(index[:, None] <= index[None, :], upper, upper.T)
    return jnp.where(index[:, None] == index[None, :], 1, mirrored).astype(jnp.int32)


def with_ends(drawn, stream_key, low, high):
    extent = drawn.shape
    spot = [jax.random.randint(jax.random.fold_in(stream_key, axis), (), 0, extent[axis]) for axis in range(len(extent))]
    drawn = drawn.at[tuple(spot)].set(low)
    longest = extent.index(max(extent))
    spot[longest] = (spot[longest] + 1) % extent[longest]
    return drawn.at[tuple(spot)].set(high)


def level_of(rng, dims, split, low, top_value):
    factor_of = 1.0
    for dim, parts in split:
        heights = jax.random.uniform(jax.random.fold_in(jax.random.fold_in(rng, 6), dim), (parts,), jnp.float32, low / len(split), top_value / len(split))
        factor_of = factor_of * jnp.repeat(jnp.exp(heights), dims[dim] // parts).reshape((-1,) + (1,) * (len(dims) - 1 - dim))
    return factor_of


def centred(stream_key, extent, scale, bound, split=(), kind=jnp.bfloat16):
    result = scale * jax.random.normal(stream_key, extent, jnp.float32)
    if split:
        result = result * level_of(stream_key, extent, split, -0.22, 0.18)
    return jnp.clip(result, -bound, bound).astype(kind)


def setup_inputs(seed: int = 0) -> dict:
    splits = jax.random.split(jax.random.key(seed), 6)
    return {
        "inv_known": draw_inv_known(jax.random.fold_in(splits[5], 71), 0),
        "pattern": draw_pattern(jax.random.fold_in(splits[5], 71), 0),
        "factor": centred(splits[2], (R, KS, W), R ** -0.5, 0.25, ((0, 32),), jnp.float32),
        "listed": with_ends((jax.random.randint(splits[3], (R, KS), 0, 4) < 3).astype(jnp.int32), jax.random.fold_in(splits[3], 1), 0, 1),
        "diag_inverse": centred(splits[4], (W, KS, W), 1.0, 6.0, ((0, 8),), jnp.float32),
    }


def reference(inv_known, pattern, factor, listed, diag_inverse):
    listed_f = listed.astype(jnp.float32)
    masked = factor * listed_f[:, :, None]
    flat = masked.reshape(R, KS * W)
    width = R // N_COL
    tiles = width // TILE

    def add_block(total, index):
        start = index * width
        cols = lax.dynamic_slice_in_dim(inv_known, start, width, 1)
        flags = lax.dynamic_slice_in_dim(pattern, index * tiles, tiles, 1).astype(jnp.float32)
        spread = jnp.repeat(jnp.repeat(flags, TILE, axis=0), TILE, axis=1)
        rows = lax.dynamic_slice_in_dim(flat, start, width, 0)
        part = jnp.dot(cols * spread, rows, precision=lax.Precision.HIGHEST, preferred_element_type=jnp.float32)
        return total + part, None

    init = jnp.zeros((R, KS * W), jnp.float32)
    total, _ = lax.scan(add_block, init, jnp.arange(N_COL, dtype=jnp.int32))
    columns = -total.reshape(R, KS, W) * listed_f[:, :, None]
    inverse_columns = jnp.transpose(columns, (2, 1, 0))
    update = jnp.einsum("ika,ikb->akb", columns, masked, precision=lax.Precision.HIGHEST)
    schur = diag_inverse - update
    return inverse_columns, schur
```

```python
import functools

import jax
import jax.numpy as jnp
from jax import lax
from jax.experimental import pallas as pl
from jax.experimental.pallas import tpu as pltpu
from jax.sharding import PartitionSpec as P

LANES = 128
CORES = 2
AXES = ("row", "col")
VMEM = pl.BlockSpec(memory_space=pltpu.VMEM)
SMEM = pl.BlockSpec(memory_space=pltpu.SMEM)


def exact(a, b, contract):
    return lax.dot_general(
        a, b, (contract, ((), ())), precision=lax.Precision.HIGHEST, preferred_element_type=jnp.float32
    )


def supernode_pass(present, masked, listed_f, diag_part, ratio):
    row_block, row_listed = (
        lax.all_gather(masked, "col", axis=0, tiled=True),
        lax.all_gather(listed_f, "col", axis=0, tiled=True),
    )
    held = lax.psum_scatter(
        jnp.einsum("ij,ika->jka", present, row_block, precision=lax.Precision.HIGHEST),
        "row",
        scatter_dimension=0,
        tiled=True,
    )
    count_row = lax.axis_size("row")
    count_col = lax.axis_size("col")
    local_rows = held.shape[0]
    nodes = held.shape[1]
    narrow = held.shape[2] // count_col
    by_column = lax.all_to_all(held[None], "col", split_axis=3, concat_axis=0, tiled=True)
    grouped = by_column.reshape(count_row, 1, ratio, local_rows, nodes, narrow)
    moved = lax.all_to_all(grouped, "row", split_axis=0, concat_axis=1, tiled=True)
    ordered = jnp.transpose(moved[0], (1, 0, 2, 3, 4)).reshape(
        ratio * count_row * local_rows, nodes, narrow
    )
    summed = jnp.transpose(ordered, (2, 1, 0))
    columns = -summed * jnp.transpose(row_listed)[None, :, :]
    update = jnp.einsum("akj,jkb->akb", columns, row_block, precision=lax.Precision.HIGHEST)
    schur = diag_part - lax.psum(update, "row")
    return (columns, schur)


def general(inv_known, pattern, factor, listed, diag_inverse):
    tile = inv_known.shape[0] // pattern.shape[0]
    flags = pattern.astype(jnp.float32)
    spread = jnp.repeat(jnp.repeat(flags, tile, axis=0), tile, axis=1)
    present = inv_known * spread
    listed_f = listed.astype(jnp.float32)
    masked = factor * listed_f[:, :, None]
    ratio = lax.axis_size("col") // lax.axis_size("row")
    return supernode_pass(present, masked, listed_f, diag_inverse, ratio)


class Sizes:
    def __init__(self, inv_known, pattern, factor, diag_inverse):
        self.n_row = lax.axis_size("row")
        self.n_col = lax.axis_size("col")
        self.n_z = self.n_col // CORES
        self.own = factor.shape[0]
        self.nodes = factor.shape[1]
        self.width = factor.shape[2]
        self.tiles = self.width // LANES
        self.slots = self.tiles * self.nodes
        self.rows_r = inv_known.shape[0]
        self.rows_c = inv_known.shape[1]
        self.wide = diag_inverse.shape[0]
        self.pattern = pattern.shape
        self.span = self.n_col * self.own
        self.m_rows = self.own * self.slots
        self.bulk = self.m_rows + self.rows_c + 8
        self.small = self.nodes * self.own
        self.total = self.n_row * self.rows_r

    def fits(self):
        def power(n):
            return n > 0 and n & (n - 1) == 0

        return (
            self.n_col % CORES == 0
            and power(self.n_row)
            and power(self.n_z)
            and self.n_row > 1
            and self.wide * CORES == LANES
            and self.rows_r == LANES
            and self.span == LANES
            and self.width % LANES == 0
            and self.slots % 8 == 0
            and self.own % 8 == 0
            and self.rows_c % 8 == 0
            and self.nodes <= 8
        )


def spot():
    r = lax.axis_index("row")
    c = lax.axis_index("col")
    return r, lax.div(c, CORES), lax.rem(c, CORES)


def pack_kernel(n, factor, listed, inv_t, pattern, bulk, *smalls):
    r, z, core = spot()
    col = z * CORES + core
    line = lax.broadcasted_iota(jnp.int32, (n.slots, LANES), 0)
    head = lax.broadcasted_iota(jnp.int32, (8, LANES), 0)
    lane8 = lax.broadcasted_iota(jnp.int32, (8, LANES), 1)
    flags = jnp.zeros((8, LANES), jnp.float32)
    for m in range(n.own):
        keep = jnp.zeros((n.slots, LANES), jnp.float32)
        for k in range(n.nodes):
            value = listed[m, k].astype(jnp.float32)
            keep = jnp.where(lax.rem(line, n.nodes) == k, value, keep)
            flags = jnp.where((head == k) & (lane8 == col * n.own + m), value, flags)
        part = pl.ds(m * n.slots, n.slots)
        bulk[part, :] = factor[part, :] * keep
    bulk[pl.ds(n.m_rows + n.rows_c, 8), :] = flags
    high = n.rows_r // n.pattern[0]
    deep = n.rows_c // n.pattern[1]
    lane = lax.broadcasted_iota(jnp.int32, (deep, LANES), 1)
    for q in range(n.pattern[1]):
        keep = jnp.zeros((deep, LANES), jnp.float32)
        for p in range(n.pattern[0]):
            keep = jnp.where(lax.div(lane, high) == p, pattern[p, q].astype(jnp.float32), keep)
        bulk[pl.ds(n.m_rows + q * deep, deep), :] = inv_t[pl.ds(q * deep, deep), :] * keep
    for k in range(n.nodes):
        loads = [bulk[pl.ds(t * n.nodes + k, n.own, stride=n.slots), :] for t in range(n.tiles)]
        for s, small in enumerate(smalls):
            want = z ^ s
            piece = loads[0]
            for t in range(1, n.tiles):
                piece = jnp.where(want == t, loads[t], piece)
            small[pl.ds(k * n.own, n.own), :] = piece


def stack_kernel(n, *refs):
    out = refs[-1]
    for s, ref in enumerate(refs[:-1]):
        out[pl.ds(s * n.small, n.small), :] = ref[...]


def work_kernel(n, *refs):
    smalls = refs[: CORES * n.n_row]
    bulks = refs[CORES * n.n_row : CORES * (n.n_row + n.n_z)]
    columns, update, m_all, m_row, p_t, x_t = refs[CORES * (n.n_row + n.n_z) :]
    r, z, core = spot()
    mask = jnp.zeros((8, LANES), jnp.float32)
    for q in range(CORES):
        for s in range(n.n_z):
            ref = bulks[q * n.n_z + s]
            c = (z ^ s) * CORES + (core ^ q)
            m_row[pl.ds(c * n.m_rows, n.m_rows), :] = ref[pl.ds(0, n.m_rows), :]
            p_t[pl.ds(c * n.rows_c, n.rows_c), :] = ref[pl.ds(n.m_rows, n.rows_c), :]
            mask += ref[pl.ds(n.m_rows + n.rows_c, 8), :]
        for d in range(n.n_row):
            ref = smalls[q * n.n_row + d]
            for s in range(n.n_z):
                c = (z ^ s) * CORES + (core ^ q)
                at = (r ^ d) * n.span + c * n.own
                for k in range(n.nodes):
                    m_all[k, pl.ds(at, n.own), :] = ref[pl.ds(s * n.small + k * n.own, n.own), :]
    for k in range(n.nodes):
        x_t[k] = exact(m_all[k], p_t[...], ((0,), (0,)))
        part = -x_t[k, pl.ds(core * n.wide, n.wide), :] * mask[k : k + 1, :]
        columns[pl.ds(k, n.wide, stride=n.nodes), :] = part
        for t in range(n.tiles):
            side = m_row[pl.ds(t * n.nodes + k, n.rows_r, stride=n.slots), :]
            update[pl.ds(t * n.nodes + k, n.wide, stride=n.slots), :] = exact(part, side, ((1,), (0,)))


def fast(n, inv_known, pattern, factor, listed, diag_inverse):
    def shape(*dims):
        return jax.ShapeDtypeStruct(dims, jnp.float32)

    def route(array, change):
        pairs = []
        for r in range(n.n_row):
            for z in range(n.n_z):
                for core in range(CORES):
                    r2, z2, core2 = change(r, z, core)
                    pairs.append(((r * n.n_z + z) * CORES + core, (r2 * n.n_z + z2) * CORES + core2))
        return lax.ppermute(array, AXES, pairs)

    def over_z(array, s):
        return route(array, lambda r, z, core: (r, z ^ s, core))

    def over_row(array, d):
        return route(array, lambda r, z, core: (r ^ d, z, core))

    def over_core(array):
        return route(array, lambda r, z, core: (r, z, core ^ 1))

    steps = [1 << i for i in range(n.n_row.bit_length() - 1)]

    def over_pair(array, i):
        return route(array, lambda r, z, core: (r ^ (steps[i] if core == 0 else steps[-1 - i]), z, core))

    def view(array):
        lead = array.shape[0]
        split = array.reshape(lead, n.nodes, n.tiles, LANES)
        return jnp.transpose(split, (0, 2, 1, 3)).reshape(lead * n.slots, LANES)

    bulk, *smalls = pl.pallas_call(
        functools.partial(pack_kernel, n),
        in_specs=[VMEM, SMEM, VMEM, SMEM],
        out_specs=[VMEM] * (1 + n.n_z),
        out_shape=[shape(n.bulk, LANES)] + [shape(n.small, LANES)] * n.n_z,
    )(view(factor), listed, inv_known.T, pattern)

    smalls = [smalls[0]] + [over_z(smalls[s], s) for s in range(1, n.n_z)]
    bulks = [bulk] + [over_z(bulk, s) for s in range(1, n.n_z)]
    small = pl.pallas_call(
        functools.partial(stack_kernel, n),
        in_specs=[VMEM] * n.n_z,
        out_specs=VMEM,
        out_shape=shape(n.n_z * n.small, LANES),
    )(*smalls)
    spread = [small] + [over_row(small, d) for d in range(1, n.n_row)]
    other_bulks = [over_core(b) for b in bulks]
    other_spread = [over_core(b) for b in spread]
    columns, update = pl.pallas_call(
        functools.partial(work_kernel, n),
        in_specs=[VMEM] * (CORES * (n.n_row + n.n_z)),
        out_specs=[VMEM] * 2,
        out_shape=[shape(n.wide * n.nodes, LANES), shape(n.wide * n.slots, LANES)],
        scratch_shapes=[
            pltpu.VMEM((n.nodes, n.total, LANES), jnp.float32),
            pltpu.VMEM((n.span * n.slots, LANES), jnp.float32),
            pltpu.VMEM((n.total, LANES), jnp.float32),
            pltpu.VMEM((n.nodes, LANES, LANES), jnp.float32),
        ],
    )(*spread, *other_spread, *bulks, *other_bulks)
    for i in range(len(steps)):
        update = update + over_pair(update, i)
    schur = view(diag_inverse) - update
    schur = jnp.transpose(schur.reshape(n.wide, n.tiles, n.nodes, LANES), (0, 2, 1, 3))
    return columns.reshape(n.wide, n.nodes, LANES), schur.reshape(n.wide, n.nodes, n.width)


def local(inv_known, pattern, factor, listed, diag_inverse):
    n = Sizes(inv_known, pattern, factor, diag_inverse)
    plan = functools.partial(fast, n) if n.fits() else general
    return plan(inv_known, pattern, factor, listed, diag_inverse)


def solution(mesh):
    in_specs = (
        P("row", "col"),
        P("row", "col"),
        P(("row", "col"), None, None),
        P(("row", "col"), None),
        P("col", None, None),
    )
    out_specs = (P("col", None, "row"), P("col", None, None))
    return jax.shard_map(local, mesh=mesh, in_specs=in_specs, out_specs=out_specs, check_vma=False)
```

```python
import functools
import math

import jax
import jax.numpy as jnp
from jax import lax
from jax.experimental import pallas as pl
from jax.experimental.pallas import tpu as pltpu
from jax.sharding import PartitionSpec as P

LANES = 128
CORES = 2
CHUNKS = 2
AXES = ("row", "col")
VMEM = pl.BlockSpec(memory_space=pltpu.VMEM)


def room(*arrays):
    return pltpu.CompilerParams(vmem_limit_bytes=8 * sum(math.prod(a.shape) for a in arrays) + (1 << 20))


def cheap():
    return pl.CostEstimate(flops=1, bytes_accessed=1, transcendentals=0)


def exact(a, b, contract):
    return lax.dot_general(
        a, b, (contract, ((), ())), precision=lax.Precision.HIGHEST, preferred_element_type=jnp.float32
    )


def supernode_pass(present, masked, listed_f, diag_part, ratio):
    row_block, row_listed = (
        lax.all_gather(masked, "col", axis=0, tiled=True),
        lax.all_gather(listed_f, "col", axis=0, tiled=True),
    )
    held = lax.psum_scatter(
        jnp.einsum("ij,ika->jka", present, row_block, precision=lax.Precision.HIGHEST),
        "row",
        scatter_dimension=0,
        tiled=True,
    )
    count_row = lax.axis_size("row")
    count_col = lax.axis_size("col")
    local_rows = held.shape[0]
    nodes = held.shape[1]
    narrow = held.shape[2] // count_col
    by_column = lax.all_to_all(held[None], "col", split_axis=3, concat_axis=0, tiled=True)
    grouped = by_column.reshape(count_row, 1, ratio, local_rows, nodes, narrow)
    moved = lax.all_to_all(grouped, "row", split_axis=0, concat_axis=1, tiled=True)
    ordered = jnp.transpose(moved[0], (1, 0, 2, 3, 4)).reshape(
        ratio * count_row * local_rows, nodes, narrow
    )
    summed = jnp.transpose(ordered, (2, 1, 0))
    columns = -summed * jnp.transpose(row_listed)[None, :, :]
    update = jnp.einsum("akj,jkb->akb", columns, row_block, precision=lax.Precision.HIGHEST)
    schur = diag_part - lax.psum(update, "row")
    return (columns, schur)


def general(inv_known, pattern, factor, listed, diag_inverse):
    tile = inv_known.shape[0] // pattern.shape[0]
    flags = pattern.astype(jnp.float32)
    spread = jnp.repeat(jnp.repeat(flags, tile, axis=0), tile, axis=1)
    present = inv_known * spread
    listed_f = listed.astype(jnp.float32)
    masked = factor * listed_f[:, :, None]
    ratio = lax.axis_size("col") // lax.axis_size("row")
    return supernode_pass(present, masked, listed_f, diag_inverse, ratio)


class Sizes:
    def __init__(self, inv_known, pattern, factor, diag_inverse):
        self.n_row = lax.axis_size("row")
        self.n_col = lax.axis_size("col")
        self.n_z = self.n_col // CORES
        self.own = factor.shape[0]
        self.nodes = factor.shape[1]
        self.width = factor.shape[2]
        self.tiles = self.width // LANES
        self.slots = self.tiles * self.nodes
        self.rows_r = inv_known.shape[0]
        self.rows_c = inv_known.shape[1]
        self.wide = diag_inverse.shape[0]
        self.pattern = pattern.shape
        self.span = self.n_col * self.own
        self.m_rows = self.own * self.slots
        self.bulk = self.m_rows + self.rows_c + 8
        self.small = self.nodes * self.own
        self.total = self.n_row * self.rows_r
        far = range(CORES, self.n_z)
        self.pairs = [tuple(far[i : i + CORES]) for i in range(0, len(far), CORES)]

    def fits(self):
        def power(n):
            return n > 0 and n & (n - 1) == 0

        return (
            self.n_col % CORES == 0
            and power(self.n_row)
            and power(self.n_z)
            and self.n_row > 1
            and self.n_z > 1
            and self.wide * CORES == LANES
            and self.rows_r == LANES
            and self.span == LANES
            and self.width % LANES == 0
            and self.slots % 8 == 0
            and self.own % 8 == 0
            and self.rows_c % 8 == 0
            and self.nodes % CORES == 0
            and self.nodes <= 8
            and self.wide % (8 * CHUNKS) == 0
        )


def spot():
    r = lax.axis_index("row")
    c = lax.axis_index("col")
    return r, lax.div(c, CORES), lax.rem(c, CORES)


def pack_kernel(n, factor_h, listed_h, inv_h, pattern_h, bulk, *rest):
    smalls = rest[: n.n_z - 1]
    factor, listed_t, inv_t, pattern_t, wide_l, sems = rest[n.n_z - 1 :]
    pairs = ((factor_h, factor), (listed_h, listed_t), (inv_h, inv_t), (pattern_h, pattern_t))
    copies = [pltpu.make_async_copy(a, b, sems.at[i]) for i, (a, b) in enumerate(pairs)]
    for copy in copies:
        copy.start()
    for copy in copies:
        copy.wait()
    _, z, core = spot()
    col = z * CORES + core
    wide_l[...] = jnp.zeros((8, LANES), jnp.float32)
    wide_l[pl.ds(0, n.nodes), pl.ds(0, n.own)] = listed_t[...].astype(jnp.float32)
    flags = wide_l[...]
    row = lax.broadcasted_iota(jnp.int32, (n.m_rows, LANES), 0)
    lane = lax.broadcasted_iota(jnp.int32, (n.m_rows, LANES), 1)
    node = lax.rem(row, n.nodes)
    mine = jnp.zeros((n.m_rows, LANES), jnp.float32)
    for k in range(n.nodes):
        mine = jnp.where(node == k, flags[k : k + 1, :], mine)
    keep = jnp.sum(jnp.where(lane == lax.div(row, n.slots), mine, 0.0), axis=1, keepdims=True)
    bulk[pl.ds(0, n.m_rows), :] = factor[...] * keep
    bulk[pl.ds(n.m_rows + n.rows_c, 8), :] = pltpu.roll(flags, col * n.own, 1)
    high = n.rows_r // n.pattern[0]
    deep = n.rows_c // n.pattern[1]
    tile = lax.div(lax.broadcasted_iota(jnp.int32, (1, LANES), 1), high)
    for q in range(n.pattern[1]):
        keep = jnp.zeros((1, LANES), jnp.float32)
        for p in range(n.pattern[0]):
            keep = jnp.where(tile == p, pattern_t[q : q + 1, p : p + 1].astype(jnp.float32), keep)
        bulk[pl.ds(n.m_rows + q * deep, deep), :] = inv_t[pl.ds(q * deep, deep), :] * keep
    for s, small in zip((0, *range(CORES, n.n_z)), smalls):
        cut(n, bulk, z ^ s, small, 0)


def cut(n, bulk, want, out, at):
    for k in range(n.nodes):
        piece = None
        for t in range(n.tiles):
            load = bulk[pl.ds(t * n.nodes + k, n.own, stride=n.slots), :]
            piece = load if piece is None else jnp.where(want == t, load, piece)
        out[pl.ds(at + k * n.own, n.own), :] = piece


def stack_kernel(n, own, bulk, *refs):
    out = refs[-1]
    _, z, _ = spot()
    out[pl.ds(0, n.small), :] = own[...]
    cut(n, bulk, z, out, n.small)
    for s, ref in enumerate(refs[:-1]):
        out[pl.ds((s + CORES) * n.small, n.small), :] = ref[...]


def join_kernel(n, *refs):
    out = refs[-1]
    at = 0
    for ref in refs[:-1]:
        out[pl.ds(at, ref.shape[0]), :] = ref[...]
        at += ref.shape[0]


def choose(core, pair):
    return jnp.where(core == 0, pair[0], pair[1])


def place_kernel(n, *refs):
    half = len(refs[:-3]) // CORES
    m_row, p_t, mask_ref = refs[-3:]
    _, z, core = spot()
    mask_ref[...] = jnp.zeros((8, LANES), jnp.float32)

    def put(ref, at, c):
        m_row[pl.ds(c * n.m_rows, n.m_rows), :] = ref[pl.ds(at, n.m_rows), :]
        p_t[pl.ds(c * n.rows_c, n.rows_c), :] = ref[pl.ds(at + n.m_rows, n.rows_c), :]
        mask_ref[...] += ref[pl.ds(at + n.m_rows + n.rows_c, 8), :]

    for q in range(CORES):
        owner = core ^ q
        own, near, *rest = refs[q * half : (q + 1) * half]
        put(own, 0, z * CORES + owner)
        put(near, 0, (z ^ 1) * CORES + owner)
        for pair, ref in zip(n.pairs, rest):
            for i in range(CORES):
                put(ref, i * n.bulk, (z ^ choose(owner, pair)) * CORES + (owner ^ i))


def work_kernel(n, *refs):
    smalls = refs[:CORES]
    m_row, p_t, mask_ref, columns = refs[CORES : CORES + 4]
    *updates, m_all = refs[CORES + 4 :]
    r, z, core = spot()
    lane = lax.broadcasted_iota(jnp.int32, (n.own, LANES), 1)
    left = lane < n.wide
    first = core == 0
    for q in range(CORES):
        for d in range(n.n_row):
            for s in range(n.n_z):
                c = (z ^ s) * CORES + (core ^ q)
                at = (r ^ d) * n.span + c * n.own
                for k in range(0, n.nodes, CORES):
                    start = (d * n.n_z + s) * n.small + k * n.own
                    one = smalls[q][pl.ds(start, n.own), :]
                    two = smalls[q][pl.ds(start + n.own, n.own), :]
                    turned = pltpu.roll(jnp.where(first, two, one), n.wide, 1)
                    both = jnp.where(left == first, jnp.where(first, one, two), turned)
                    m_all[k // CORES, pl.ds(at, n.own), :] = both
    chunk = n.wide // len(updates)
    for k in range(n.nodes):
        if k % CORES == 0:
            x_t = exact(m_all[k // CORES], p_t[...], ((0,), (0,)))
        at = k % CORES * n.wide
        part = -x_t[at : at + n.wide, :] * mask_ref[k : k + 1, :]
        columns[pl.ds(k, n.wide, stride=n.nodes), :] = part
        sides = [m_row[pl.ds(t * n.nodes + k, n.rows_r, stride=n.slots), :] for t in range(n.tiles)]
        wide = exact(part, jnp.concatenate(sides, axis=1), ((1,), (0,)))
        for t in range(n.tiles):
            for h, update in enumerate(updates):
                piece = wide[h * chunk : (h + 1) * chunk, t * LANES : (t + 1) * LANES]
                update[pl.ds(t * n.nodes + k, chunk, stride=n.slots), :] = piece


def finish_kernel(h, diag, one, two, *refs):
    out, room_ref, sem = refs[-3:]
    size = one.shape[0]
    room_ref[...] = diag[pl.ds(h * size, size), :] - (one[...] + two[...])
    copy = pltpu.make_async_copy(room_ref, out.at[pl.ds(h * size, size), :], sem)
    copy.start()
    copy.wait()


def fast(n, inv_known, pattern, factor, listed, diag_inverse):
    def shape(*dims):
        return jax.ShapeDtypeStruct(dims, jnp.float32)

    def route(array, change):
        pairs = []
        for r in range(n.n_row):
            for z in range(n.n_z):
                for core in range(CORES):
                    r2, z2, core2 = change(r, z, core)
                    pairs.append(((r * n.n_z + z) * CORES + core, (r2 * n.n_z + z2) * CORES + core2))
        return lax.ppermute(array, AXES, pairs)

    def over_z(array, s):
        return route(array, lambda r, z, core: (r, z ^ s, core))

    def over_row(array, d):
        return route(array, lambda r, z, core: (r ^ d, z, core))

    def over_core(array):
        return route(array, lambda r, z, core: (r, z, core ^ 1))

    steps = [1 << i for i in range(n.n_row.bit_length() - 1)]

    def over_pair(array, i):
        return route(array, lambda r, z, core: (r ^ (steps[i] if core == 0 else steps[-1 - i]), z, core))

    def view(array):
        lead = array.shape[0]
        split = array.reshape(lead, n.nodes, n.tiles, LANES)
        return jnp.transpose(split, (0, 2, 1, 3)).reshape(lead * n.slots, LANES)

    taken = [view(factor), listed.T, inv_known.T, pattern.T]
    out = [shape(n.bulk, LANES)] + [shape(n.small, LANES)] * (n.n_z - 1)
    bulk, *smalls = pl.pallas_call(
        functools.partial(pack_kernel, n),
        in_specs=[pl.BlockSpec(memory_space=pltpu.HBM)] * 4,
        out_specs=[VMEM] * len(out),
        out_shape=out,
        scratch_shapes=[pltpu.VMEM(a.shape, a.dtype) for a in taken]
        + [pltpu.VMEM((8, LANES), jnp.float32), pltpu.SemaphoreType.DMA((len(taken),))],

        cost_estimate=cheap(),
    )(*taken)

    def join(*arrays):
        out = shape(sum(a.shape[0] for a in arrays), LANES)
        return pl.pallas_call(
            functools.partial(join_kernel, n),
            in_specs=[VMEM] * len(arrays),
            out_specs=VMEM,
            out_shape=out,
            compiler_params=room(out),
        )(*arrays)

    def over_pair_z(array, pair):
        return route(array, lambda r, z, core: (r, z ^ pair[core], core))

    near = over_z(bulk, 1)
    far = [over_z(small, s) for s, small in zip(range(CORES, n.n_z), smalls[1:])]
    other = over_core(bulk)
    both, near, far = lax.optimization_barrier((join(bulk, other), near, far))
    out = shape(n.n_z * n.small, LANES)
    small = pl.pallas_call(
        functools.partial(stack_kernel, n),
        in_specs=[VMEM] * n.n_z,
        out_specs=VMEM,
        out_shape=out,
        compiler_params=room(out),
    )(smalls[0], near, *far)
    bulks = [over_pair_z(both, pair) for pair in n.pairs]
    spread = [over_row(small, d) for d in range(1, n.n_row)]
    bulks = [bulk, near, *bulks]
    other_bulks = [other] + [over_core(b) for b in bulks[1:]]
    spread = join(small, *spread)
    spread = [spread, over_core(spread)]
    taken = [*bulks, *other_bulks]
    out = [shape(n.span * n.slots, LANES), shape(n.n_col * n.rows_c, LANES), shape(8, LANES)]
    placed = pl.pallas_call(
        functools.partial(place_kernel, n),
        in_specs=[VMEM] * len(taken),
        out_specs=[VMEM] * len(out),
        out_shape=out,
        compiler_params=room(*taken, *out),
        cost_estimate=cheap(),
    )(*taken)
    taken = [*spread, *placed]
    out = [shape(n.wide * n.nodes, LANES)] + [shape(n.wide * n.slots // CHUNKS, LANES)] * CHUNKS
    scratch = [shape(n.nodes // CORES, n.total, LANES)]
    columns, *updates = pl.pallas_call(
        functools.partial(work_kernel, n),
        in_specs=[VMEM] * len(taken),
        out_specs=[VMEM] * len(out),
        out_shape=out,
        scratch_shapes=[pltpu.VMEM(a.shape, a.dtype) for a in scratch],
        compiler_params=room(*taken, *out, *scratch),
        cost_estimate=cheap(),
    )(*taken)
    for i in range(len(steps) - 1):
        updates = [update + over_pair(update, i) for update in updates]
    got = [over_pair(update, len(steps) - 1) for update in updates]
    diag = view(diag_inverse)
    schur = None
    for h, pair in enumerate(zip(updates, got)):
        taken = [diag, *pair] + ([] if schur is None else [schur])
        schur = pl.pallas_call(
            functools.partial(finish_kernel, h),
            in_specs=[VMEM] * 3 + [pl.BlockSpec(memory_space=pl.ANY)] * (len(taken) - 3),
            out_specs=pl.BlockSpec(memory_space=pl.ANY),
            out_shape=shape(n.wide * n.slots, LANES),
            scratch_shapes=[pltpu.VMEM(pair[0].shape, jnp.float32), pltpu.SemaphoreType.DMA],
            input_output_aliases={} if schur is None else {3: 0},
            compiler_params=room(*taken),
        )(*taken)
    schur = jnp.transpose(schur.reshape(n.wide, n.tiles, n.nodes, LANES), (0, 2, 1, 3))
    return columns.reshape(n.wide, n.nodes, LANES), schur.reshape(n.wide, n.nodes, n.width)


def local(inv_known, pattern, factor, listed, diag_inverse):
    n = Sizes(inv_known, pattern, factor, diag_inverse)
    plan = functools.partial(fast, n) if n.fits() else general
    return plan(inv_known, pattern, factor, listed, diag_inverse)


def solution(mesh):
    in_specs = (
        P("row", "col"),
        P("row", "col"),
        P(("row", "col"), None, None),
        P(("row", "col"), None),
        P("col", None, None),
    )
    out_specs = (P("col", None, "row"), P("col", None, None))
    return jax.shard_map(local, mesh=mesh, in_specs=in_specs, out_specs=out_specs, check_vma=False)
```

```python
import functools
import math

import jax
import jax.numpy as jnp
from jax import lax
from jax.experimental import pallas as pl
from jax.experimental.pallas import tpu as pltpu
from jax.sharding import PartitionSpec as P

LANES = 128
CORES = 2
CHUNKS = 2
AXES = ("row", "col")
VMEM = pl.BlockSpec(memory_space=pltpu.VMEM)


def room(*arrays):
    return pltpu.CompilerParams(vmem_limit_bytes=8 * sum(math.prod(a.shape) for a in arrays) + (1 << 20))


def exact(a, b, contract):
    return lax.dot_general(
        a, b, (contract, ((), ())), precision=lax.Precision.HIGHEST, preferred_element_type=jnp.float32
    )


def supernode_pass(present, masked, listed_f, diag_part, ratio):
    row_block, row_listed = (
        lax.all_gather(masked, "col", axis=0, tiled=True),
        lax.all_gather(listed_f, "col", axis=0, tiled=True),
    )
    held = lax.psum_scatter(
        jnp.einsum("ij,ika->jka", present, row_block, precision=lax.Precision.HIGHEST),
        "row",
        scatter_dimension=0,
        tiled=True,
    )
    count_row = lax.axis_size("row")
    count_col = lax.axis_size("col")
    local_rows = held.shape[0]
    nodes = held.shape[1]
    narrow = held.shape[2] // count_col
    by_column = lax.all_to_all(held[None], "col", split_axis=3, concat_axis=0, tiled=True)
    grouped = by_column.reshape(count_row, 1, ratio, local_rows, nodes, narrow)
    moved = lax.all_to_all(grouped, "row", split_axis=0, concat_axis=1, tiled=True)
    ordered = jnp.transpose(moved[0], (1, 0, 2, 3, 4)).reshape(
        ratio * count_row * local_rows, nodes, narrow
    )
    summed = jnp.transpose(ordered, (2, 1, 0))
    columns = -summed * jnp.transpose(row_listed)[None, :, :]
    update = jnp.einsum("akj,jkb->akb", columns, row_block, precision=lax.Precision.HIGHEST)
    schur = diag_part - lax.psum(update, "row")
    return (columns, schur)


def general(inv_known, pattern, factor, listed, diag_inverse):
    tile = inv_known.shape[0] // pattern.shape[0]
    flags = pattern.astype(jnp.float32)
    spread = jnp.repeat(jnp.repeat(flags, tile, axis=0), tile, axis=1)
    present = inv_known * spread
    listed_f = listed.astype(jnp.float32)
    masked = factor * listed_f[:, :, None]
    ratio = lax.axis_size("col") // lax.axis_size("row")
    return supernode_pass(present, masked, listed_f, diag_inverse, ratio)


class Sizes:
    def __init__(self, inv_known, pattern, factor, diag_inverse):
        self.n_row = lax.axis_size("row")
        self.n_col = lax.axis_size("col")
        self.n_z = self.n_col // CORES
        self.own = factor.shape[0]
        self.nodes = factor.shape[1]
        self.width = factor.shape[2]
        self.tiles = self.width // LANES
        self.slots = self.tiles * self.nodes
        self.rows_r = inv_known.shape[0]
        self.rows_c = inv_known.shape[1]
        self.wide = diag_inverse.shape[0]
        self.pattern = pattern.shape
        self.span = self.n_col * self.own
        self.m_rows = self.own * self.slots
        self.bulk = self.m_rows + self.rows_c + 8
        self.small = self.nodes * self.own
        self.total = self.n_row * self.rows_r
        far = range(CORES, self.n_z)
        self.pairs = [tuple(far[i : i + CORES]) for i in range(0, len(far), CORES)]

    def fits(self):
        def power(n):
            return n > 0 and n & (n - 1) == 0

        return (
            self.n_col % CORES == 0
            and power(self.n_row)
            and power(self.n_z)
            and self.n_row > 1
            and self.n_z > 1
            and self.wide * CORES == LANES
            and self.rows_r == LANES
            and self.span == LANES
            and self.width % LANES == 0
            and self.slots % 8 == 0
            and self.own % 8 == 0
            and self.rows_c % 8 == 0
            and self.nodes % CORES == 0
            and self.nodes <= 8
            and self.wide % (8 * CHUNKS) == 0
        )


def spot():
    r = lax.axis_index("row")
    c = lax.axis_index("col")
    return r, lax.div(c, CORES), lax.rem(c, CORES)


def pack_kernel(n, factor_h, listed_h, inv_h, pattern_h, bulk, small, factor, listed_t, inv_t, pattern_t, wide_l, sems):
    pairs = ((factor_h, factor), (listed_h, listed_t), (inv_h, inv_t), (pattern_h, pattern_t))
    copies = [pltpu.make_async_copy(a, b, sems.at[i]) for i, (a, b) in enumerate(pairs)]
    for copy in copies:
        copy.start()
    for copy in copies:
        copy.wait()
    _, z, core = spot()
    col = z * CORES + core
    wide_l[...] = jnp.zeros((8, LANES), jnp.float32)
    wide_l[pl.ds(0, n.nodes), pl.ds(0, n.own)] = listed_t[...].astype(jnp.float32)
    flags = wide_l[...]
    row = lax.broadcasted_iota(jnp.int32, (n.m_rows, LANES), 0)
    lane = lax.broadcasted_iota(jnp.int32, (n.m_rows, LANES), 1)
    node = lax.rem(row, n.nodes)
    mine = jnp.zeros((n.m_rows, LANES), jnp.float32)
    for k in range(n.nodes):
        mine = jnp.where(node == k, flags[k : k + 1, :], mine)
    keep = jnp.sum(jnp.where(lane == lax.div(row, n.slots), mine, 0.0), axis=1, keepdims=True)
    bulk[pl.ds(0, n.m_rows), :] = factor[...] * keep
    bulk[pl.ds(n.m_rows + n.rows_c, 8), :] = pltpu.roll(flags, col * n.own, 1)
    high = n.rows_r // n.pattern[0]
    deep = n.rows_c // n.pattern[1]
    tile = lax.div(lax.broadcasted_iota(jnp.int32, (1, LANES), 1), high)
    for q in range(n.pattern[1]):
        keep = jnp.zeros((1, LANES), jnp.float32)
        for p in range(n.pattern[0]):
            keep = jnp.where(tile == p, pattern_t[q : q + 1, p : p + 1].astype(jnp.float32), keep)
        bulk[pl.ds(n.m_rows + q * deep, deep), :] = inv_t[pl.ds(q * deep, deep), :] * keep
    cut(n, bulk, 0, z, small, 0)


def choose(core, pair):
    return jnp.where(core == 0, pair[0], pair[1])


def cut(n, bulk, start, want, out, at):
    for k in range(n.nodes):
        piece = None
        for t in range(n.tiles):
            load = bulk[pl.ds(start + t * n.nodes + k, n.own, stride=n.slots), :]
            piece = load if piece is None else jnp.where(want == t, load, piece)
        out[pl.ds(at + k * n.own, n.own), :] = piece


def both_kernel(n, bulk, other, both, *smalls):
    _, z, core = spot()
    both[pl.ds(0, n.bulk), :] = bulk[...]
    both[pl.ds(n.bulk, n.bulk), :] = other[...]
    for pair, small in zip(n.pairs, smalls):
        for i in range(CORES):
            cut(n, both, i * n.bulk, z ^ choose(core, pair), small, i * n.small)


def stack_kernel(n, own, bulk, *refs):
    out = refs[-1]
    _, z, _ = spot()
    out[pl.ds(0, n.small), :] = own[...]
    cut(n, bulk, 0, z, out, n.small)
    for p, ref in enumerate(refs[:-1]):
        out[pl.ds((p + 1) * CORES * n.small, CORES * n.small), :] = ref[...]


def join_kernel(n, *refs):
    out = refs[-1]
    at = 0
    for ref in refs[:-1]:
        out[pl.ds(at, ref.shape[0]), :] = ref[...]
        at += ref.shape[0]


def slots(n, z, owner):
    found = [(z, owner), (z ^ 1, owner)]
    for pair in n.pairs:
        found += [(z ^ choose(owner, pair), owner ^ i) for i in range(CORES)]
    return [a * CORES + b for a, b in found]


def work_kernel(n, mine, theirs, bulk, other, columns, *refs):
    *updates, m_all, m_row, p_t, mask_ref = refs
    r, z, core = spot()
    mask_ref[...] = jnp.zeros((8, LANES), jnp.float32)

    def put(ref, at, c):
        m_row[pl.ds(c * n.m_rows, n.m_rows), :] = ref[pl.ds(at, n.m_rows), :]
        p_t[pl.ds(c * n.rows_c, n.rows_c), :] = ref[pl.ds(at + n.m_rows, n.rows_c), :]
        mask_ref[...] += ref[pl.ds(at + n.m_rows + n.rows_c, 8), :]

    lane = lax.broadcasted_iota(jnp.int32, (n.own, LANES), 1)
    left = lane < n.wide
    first = core == 0
    head = n.n_row * n.n_z * n.small
    for ref, own, owner in ((mine, bulk, core), (theirs, other, core ^ 1)):
        for s, c in enumerate(slots(n, z, owner)):
            if s == 0:
                put(own, 0, c)
            else:
                put(ref, head + (s - 1) * n.bulk, c)
            for d in range(n.n_row):
                at = (r ^ d) * n.span + c * n.own
                for k in range(0, n.nodes, CORES):
                    start = (d * n.n_z + s) * n.small + k * n.own
                    one = ref[pl.ds(start, n.own), :]
                    two = ref[pl.ds(start + n.own, n.own), :]
                    turned = pltpu.roll(jnp.where(first, two, one), n.wide, 1)
                    both = jnp.where(left == first, jnp.where(first, one, two), turned)
                    m_all[k // CORES, pl.ds(at, n.own), :] = both
    chunk = n.wide // len(updates)
    for k in range(n.nodes):
        if k % CORES == 0:
            x_t = exact(m_all[k // CORES], p_t[...], ((0,), (0,)))
        at = k % CORES * n.wide
        part = -x_t[at : at + n.wide, :] * mask_ref[k : k + 1, :]
        columns[pl.ds(k, n.wide, stride=n.nodes), :] = part
        sides = [m_row[pl.ds(t * n.nodes + k, n.rows_r, stride=n.slots), :] for t in range(n.tiles)]
        wide = exact(part, jnp.concatenate(sides, axis=1), ((1,), (0,)))
        for t in range(n.tiles):
            for h, update in enumerate(updates):
                piece = wide[h * chunk : (h + 1) * chunk, t * LANES : (t + 1) * LANES]
                update[pl.ds(t * n.nodes + k, chunk, stride=n.slots), :] = piece


def finish_kernel(h, diag, one, two, *refs):
    out, room_ref, sem = refs[-3:]
    size = one.shape[0]
    room_ref[...] = diag[pl.ds(h * size, size), :] - (one[...] + two[...])
    copy = pltpu.make_async_copy(room_ref, out.at[pl.ds(h * size, size), :], sem)
    copy.start()
    copy.wait()


def fast(n, inv_known, pattern, factor, listed, diag_inverse):
    def shape(*dims):
        return jax.ShapeDtypeStruct(dims, jnp.float32)

    def route(array, change):
        pairs = []
        for r in range(n.n_row):
            for z in range(n.n_z):
                for core in range(CORES):
                    r2, z2, core2 = change(r, z, core)
                    pairs.append(((r * n.n_z + z) * CORES + core, (r2 * n.n_z + z2) * CORES + core2))
        return lax.ppermute(array, AXES, pairs)

    def over_z(array, s):
        return route(array, lambda r, z, core: (r, z ^ s, core))

    def over_row(array, d):
        return route(array, lambda r, z, core: (r ^ d, z, core))

    def over_core(array):
        return route(array, lambda r, z, core: (r, z, core ^ 1))

    steps = [1 << i for i in range(n.n_row.bit_length() - 1)]

    def over_pair(array, i):
        return route(array, lambda r, z, core: (r ^ (steps[i] if core == 0 else steps[-1 - i]), z, core))

    def view(array):
        lead = array.shape[0]
        split = array.reshape(lead, n.nodes, n.tiles, LANES)
        return jnp.transpose(split, (0, 2, 1, 3)).reshape(lead * n.slots, LANES)

    taken = [pltpu.with_memory_space_constraint(a, pltpu.HBM) for a in (view(factor), listed.T, inv_known.T, pattern.T)]
    out = [shape(n.bulk, LANES), shape(n.small, LANES)]
    bulk, own_small = pl.pallas_call(
        functools.partial(pack_kernel, n),
        in_specs=[pl.BlockSpec(memory_space=pltpu.HBM)] * 4,
        out_specs=[VMEM] * 2,
        out_shape=out,
        scratch_shapes=[pltpu.VMEM(a.shape, a.dtype) for a in taken]
        + [pltpu.VMEM((8, LANES), jnp.float32), pltpu.SemaphoreType.DMA((len(taken),))],
        compiler_params=room(*out, *taken),
    )(*taken)

    def join(*arrays):
        out = shape(sum(a.shape[0] for a in arrays), LANES)
        return pl.pallas_call(
            functools.partial(join_kernel, n),
            in_specs=[VMEM] * len(arrays),
            out_specs=VMEM,
            out_shape=out,
            compiler_params=room(out),
        )(*arrays)

    def over_pair_z(array, pair):
        return route(array, lambda r, z, core: (r, z ^ pair[core], core))

    near = over_z(bulk, 1)
    other = over_core(bulk)
    out = [shape(CORES * n.bulk, LANES)] + [shape(CORES * n.small, LANES)] * len(n.pairs)
    both, *far = pl.pallas_call(
        functools.partial(both_kernel, n),
        in_specs=[VMEM] * 2,
        out_specs=[VMEM] * len(out),
        out_shape=out,
        compiler_params=room(*out),
    )(bulk, other)
    far = [over_pair_z(small, pair) for small, pair in zip(far, n.pairs)]
    both, near, far = lax.optimization_barrier((both, near, far))
    out = shape(n.n_z * n.small, LANES)
    small = pl.pallas_call(
        functools.partial(stack_kernel, n),
        in_specs=[VMEM] * (2 + len(far)),
        out_specs=VMEM,
        out_shape=out,
        compiler_params=room(out),
    )(own_small, near, *far)
    bulks = [over_pair_z(both, pair) for pair in n.pairs]
    spread = [over_row(small, d) for d in range(1, n.n_row)]
    mine = join(small, *spread, near, *bulks)
    taken = [mine, over_core(mine), bulk, other]
    out = [shape(n.wide * n.nodes, LANES)] + [shape(n.wide * n.slots // CHUNKS, LANES)] * CHUNKS
    scratch = [
        shape(n.nodes // CORES, n.total, LANES),
        shape(n.span * n.slots, LANES),
        shape(n.n_col * n.rows_c, LANES),
        shape(8, LANES),
    ]
    columns, *updates = pl.pallas_call(
        functools.partial(work_kernel, n),
        in_specs=[VMEM] * len(taken),
        out_specs=[VMEM] * len(out),
        out_shape=out,
        scratch_shapes=[pltpu.VMEM(a.shape, a.dtype) for a in scratch],
        compiler_params=room(*taken, *out, *scratch),
    )(*taken)
    for i in range(len(steps) - 1):
        updates = [update + over_pair(update, i) for update in updates]
    got = [over_pair(update, len(steps) - 1) for update in updates]
    diag = view(diag_inverse)
    schur = None
    for h, pair in enumerate(zip(updates, got)):
        taken = [diag, *pair] + ([] if schur is None else [schur])
        schur = pl.pallas_call(
            functools.partial(finish_kernel, h),
            in_specs=[VMEM] * 3 + [pl.BlockSpec(memory_space=pl.ANY)] * (len(taken) - 3),
            out_specs=pl.BlockSpec(memory_space=pl.ANY),
            out_shape=shape(n.wide * n.slots, LANES),
            scratch_shapes=[pltpu.VMEM(pair[0].shape, jnp.float32), pltpu.SemaphoreType.DMA],
            input_output_aliases={} if schur is None else {3: 0},
            compiler_params=room(*taken),
        )(*taken)
    schur = jnp.transpose(schur.reshape(n.wide, n.tiles, n.nodes, LANES), (0, 2, 1, 3))
    return columns.reshape(n.wide, n.nodes, LANES), schur.reshape(n.wide, n.nodes, n.width)


def local(inv_known, pattern, factor, listed, diag_inverse):
    n = Sizes(inv_known, pattern, factor, diag_inverse)
    plan = functools.partial(fast, n) if n.fits() else general
    return plan(inv_known, pattern, factor, listed, diag_inverse)


def solution(mesh):
    in_specs = (
        P("row", "col"),
        P("row", "col"),
        P(("row", "col"), None, None),
        P(("row", "col"), None),
        P("col", None, None),
    )
    out_specs = (P("col", None, "row"), P("col", None, None))
    return jax.shard_map(local, mesh=mesh, in_specs=in_specs, out_specs=out_specs, check_vma=False)
```

```python
import functools
import math

import jax
import jax.numpy as jnp
from jax import lax
from jax.experimental import pallas as pl
from jax.experimental.pallas import tpu as pltpu
from jax.sharding import PartitionSpec as P

LANES = 128
CORES = 2
AXES = ("row", "col")
VMEM = pl.BlockSpec(memory_space=pltpu.VMEM)


def room(*arrays):
    return pltpu.CompilerParams(vmem_limit_bytes=8 * sum(math.prod(a.shape) for a in arrays) + (1 << 20))


def exact(a, b, contract):
    return lax.dot_general(
        a, b, (contract, ((), ())), precision=lax.Precision.HIGHEST, preferred_element_type=jnp.float32
    )


def halves(x):
    high = x.astype(jnp.bfloat16)
    return high, (x - high.astype(jnp.float32)).astype(jnp.bfloat16)


def product(a, b):
    (ah, al), (bh, bl) = halves(a), halves(b)

    def dot(x, y):
        return lax.dot_general(x, y, (((1,), (0,)), ((), ())), preferred_element_type=jnp.float32)

    return dot(ah, bh) + (dot(ah, bl) + dot(al, bh))


def supernode_pass(present, masked, listed_f, diag_part, ratio):
    row_block, row_listed = (
        lax.all_gather(masked, "col", axis=0, tiled=True),
        lax.all_gather(listed_f, "col", axis=0, tiled=True),
    )
    held = lax.psum_scatter(
        jnp.einsum("ij,ika->jka", present, row_block, precision=lax.Precision.HIGHEST),
        "row",
        scatter_dimension=0,
        tiled=True,
    )
    count_row = lax.axis_size("row")
    count_col = lax.axis_size("col")
    local_rows = held.shape[0]
    nodes = held.shape[1]
    narrow = held.shape[2] // count_col
    by_column = lax.all_to_all(held[None], "col", split_axis=3, concat_axis=0, tiled=True)
    grouped = by_column.reshape(count_row, 1, ratio, local_rows, nodes, narrow)
    moved = lax.all_to_all(grouped, "row", split_axis=0, concat_axis=1, tiled=True)
    ordered = jnp.transpose(moved[0], (1, 0, 2, 3, 4)).reshape(
        ratio * count_row * local_rows, nodes, narrow
    )
    summed = jnp.transpose(ordered, (2, 1, 0))
    columns = -summed * jnp.transpose(row_listed)[None, :, :]
    update = jnp.einsum("akj,jkb->akb", columns, row_block, precision=lax.Precision.HIGHEST)
    schur = diag_part - lax.psum(update, "row")
    return (columns, schur)


def general(inv_known, pattern, factor, listed, diag_inverse):
    tile = inv_known.shape[0] // pattern.shape[0]
    flags = pattern.astype(jnp.float32)
    spread = jnp.repeat(jnp.repeat(flags, tile, axis=0), tile, axis=1)
    present = inv_known * spread
    listed_f = listed.astype(jnp.float32)
    masked = factor * listed_f[:, :, None]
    ratio = lax.axis_size("col") // lax.axis_size("row")
    return supernode_pass(present, masked, listed_f, diag_inverse, ratio)


class Sizes:
    def __init__(self, inv_known, pattern, factor, diag_inverse):
        self.n_row = lax.axis_size("row")
        self.n_col = lax.axis_size("col")
        self.n_z = self.n_col // CORES
        self.own = factor.shape[0]
        self.nodes = factor.shape[1]
        self.width = factor.shape[2]
        self.tiles = self.width // LANES
        self.slots = self.tiles * self.nodes
        self.rows_r = inv_known.shape[0]
        self.rows_c = inv_known.shape[1]
        self.wide = diag_inverse.shape[0]
        self.pattern = pattern.shape
        self.span = self.n_col * self.own
        self.m_rows = self.own * self.slots
        self.bulk = self.m_rows + self.rows_c + 8
        self.total = self.n_row * self.rows_r

    def fits(self):
        return (
            self.n_col % CORES == 0
            and self.n_row == 2 * CORES
            and self.n_z == 2 * CORES
            and self.wide * CORES == LANES
            and self.rows_r == LANES
            and self.span == LANES
            and self.width % LANES == 0
            and self.slots % 8 == 0
            and self.own % 8 == 0
            and self.rows_c % 8 == 0
            and self.nodes % CORES == 0
            and self.nodes <= 8
        )


def spot():
    r = lax.axis_index("row")
    c = lax.axis_index("col")
    return r, lax.div(c, CORES), lax.rem(c, CORES)


def pack_kernel(n, factor_h, listed_h, inv_h, pattern_h, bulk, factor, listed_t, inv_t, pattern_t, wide_l, sems):
    pairs = ((factor_h, factor), (listed_h, listed_t), (inv_h, inv_t), (pattern_h, pattern_t))
    copies = [pltpu.make_async_copy(a, b, sems.at[i]) for i, (a, b) in enumerate(pairs)]
    for copy in copies:
        copy.start()
    for copy in copies:
        copy.wait()
    _, z, core = spot()
    col = z * CORES + core
    wide_l[...] = jnp.zeros((8, LANES), jnp.float32)
    wide_l[pl.ds(0, n.nodes), pl.ds(0, n.own)] = listed_t[...].astype(jnp.float32)
    flags = wide_l[...]
    row = lax.broadcasted_iota(jnp.int32, (n.m_rows, LANES), 0)
    lane = lax.broadcasted_iota(jnp.int32, (n.m_rows, LANES), 1)
    node = lax.rem(row, n.nodes)
    mine = jnp.zeros((n.m_rows, LANES), jnp.float32)
    for k in range(n.nodes):
        mine = jnp.where(node == k, flags[k : k + 1, :], mine)
    keep = jnp.sum(jnp.where(lane == lax.div(row, n.slots), mine, 0.0), axis=1, keepdims=True)
    bulk[pl.ds(0, n.m_rows), :] = factor[...] * keep
    bulk[pl.ds(n.m_rows + n.rows_c, 8), :] = pltpu.roll(flags, col * n.own, 1)
    high = n.rows_r // n.pattern[0]
    deep = n.rows_c // n.pattern[1]
    tile = lax.div(lax.broadcasted_iota(jnp.int32, (1, LANES), 1), high)
    for q in range(n.pattern[1]):
        keep = jnp.zeros((1, LANES), jnp.float32)
        for p in range(n.pattern[0]):
            keep = jnp.where(tile == p, pattern_t[q : q + 1, p : p + 1].astype(jnp.float32), keep)
        bulk[pl.ds(n.m_rows + q * deep, deep), :] = inv_t[pl.ds(q * deep, deep), :] * keep


def join_kernel(n, *refs):
    out = refs[-1]
    at = 0
    for ref in refs[:-1]:
        out[pl.ds(at, ref.shape[0]), :] = ref[...]
        at += ref.shape[0]


def cut_kernel(n, low, f_outer, s_outer, f_far, s_far, one, two):
    one[pl.ds(0, n.bulk), :] = f_outer[pl.ds(0, n.bulk), :]
    one[pl.ds(n.bulk, low), :] = f_far[pl.ds(0, low), :]
    two[pl.ds(0, n.bulk - low), :] = s_far[pl.ds(low, n.bulk - low), :]
    two[pl.ds(n.bulk - low, n.bulk), :] = s_outer[pl.ds(n.bulk, n.bulk), :]


def put(n, ref, at, r2, c2, m_all, m_sel, p_t, mask):
    _, z, core = spot()
    first = core == 0
    left = lax.broadcasted_iota(jnp.int32, (n.own, LANES), 1) < n.wide
    row = r2 * n.span + c2 * n.own
    m_all[pl.ds(row * n.slots, n.m_rows), :] = ref[pl.ds(at, n.m_rows), :]
    p_t[r2, pl.ds(c2 * n.rows_c, n.rows_c), :] = ref[pl.ds(at + n.m_rows, n.rows_c), :]
    mask[r2, c2] = ref[pl.ds(at + n.m_rows + n.rows_c, 8), :]
    for k in range(0, n.nodes, CORES):
        pair = []
        for i in range(CORES):
            piece = None
            for t in range(n.tiles):
                load = ref[pl.ds(at + t * n.nodes + k + i, n.own, stride=n.slots), :]
                piece = load if piece is None else jnp.where(z == t, load, piece)
            pair.append(piece)
        one, two = pair
        turned = pltpu.roll(jnp.where(first, two, one), n.wide, 1)
        m_sel[k // CORES, pl.ds(row, n.own), :] = jnp.where(left == first, jnp.where(first, one, two), turned)


def fill(n, pieces, mine, theirs, *refs):
    r, z, core = spot()
    for ref, owner in ((mine, core), (theirs, core ^ 1)):
        at = 0
        for shift, shells in pieces:
            for s in shells:
                put(n, ref, at, r ^ choose(owner, shift), (z ^ s) * CORES + owner, *refs)
                at += n.bulk


def fill_kernel(n, pieces, *refs):
    count = len(pieces)
    for i, group in enumerate(pieces):
        fill(n, group, refs[i], refs[count + i], *refs[2 * count :])


def work_kernel(n, pieces, mine, theirs, *refs):
    diag, columns, schur, *store = refs[4:]
    fill(n, pieces, mine, theirs, *store)
    m_all, m_sel, p_t, masks = store
    r, _, _ = spot()
    mask = []
    for i in range(n.n_row):
        total = masks[i, 0]
        for c in range(1, n.n_col):
            total += masks[i, c]
        mask.append(total)
    p_all = jnp.concatenate([p_t[i] for i in range(n.n_row)], axis=1)
    for k in range(n.nodes):
        if k % CORES == 0:
            x_t = product(m_sel[k // CORES].T, p_all)
        at = k % CORES * n.wide
        spread = jnp.concatenate([m[k : k + 1, :] for m in mask], axis=1)
        part = -x_t[at : at + n.wide, :] * spread
        own = part[:, :LANES]
        for i in range(1, n.n_row):
            own = jnp.where(r == i, part[:, i * LANES : (i + 1) * LANES], own)
        columns[pl.ds(k, n.wide, stride=n.nodes), :] = own
        sides = [m_all[pl.ds(t * n.nodes + k, n.total, stride=n.slots), :] for t in range(n.tiles)]
        wide = product(part, jnp.concatenate(sides, axis=1))
        for t in range(n.tiles):
            line = pl.ds(t * n.nodes + k, n.wide, stride=n.slots)
            schur[line, :] = diag[line, :] - wide[:, t * LANES : (t + 1) * LANES]


def choose(core, pair):
    return jnp.where(core == 0, pair[0], pair[1])


def fast(n, inv_known, pattern, factor, listed, diag_inverse):
    def shape(*dims):
        return jax.ShapeDtypeStruct(dims, jnp.float32)

    def route(array, change):
        pairs = []
        for r in range(n.n_row):
            for z in range(n.n_z):
                for core in range(CORES):
                    r2, z2, core2 = change(r, z, core)
                    pairs.append(((r * n.n_z + z) * CORES + core, (r2 * n.n_z + z2) * CORES + core2))
        return lax.ppermute(array, AXES, pairs)

    def over_z(array, s):
        return route(array, lambda r, z, core: (r, z ^ s, core))

    def over_core(array):
        return route(array, lambda r, z, core: (r, z, core ^ 1))

    steps = [1 << i for i in range(n.n_row.bit_length() - 1)]

    def over_pair(array, i):
        return route(array, lambda r, z, core: (r ^ (steps[i] if core == 0 else steps[-1 - i]), z, core))

    def view(array):
        lead = array.shape[0]
        split = array.reshape(lead, n.nodes, n.tiles, LANES)
        return jnp.transpose(split, (0, 2, 1, 3)).reshape(lead * n.slots, LANES)

    taken = [pltpu.with_memory_space_constraint(a, pltpu.HBM) for a in (view(factor), listed.T, inv_known.T, pattern.T)]
    out = shape(n.bulk, LANES)
    bulk = pl.pallas_call(
        functools.partial(pack_kernel, n),
        in_specs=[pl.BlockSpec(memory_space=pltpu.HBM)] * 4,
        out_specs=VMEM,
        out_shape=out,
        scratch_shapes=[pltpu.VMEM(a.shape, a.dtype) for a in taken]
        + [pltpu.VMEM((8, LANES), jnp.float32), pltpu.SemaphoreType.DMA((len(taken),))],
        compiler_params=room(out, *taken),
    )(*taken)

    def join(*arrays):
        out = shape(sum(a.shape[0] for a in arrays), LANES)
        return pl.pallas_call(
            functools.partial(join_kernel, n),
            in_specs=[VMEM] * len(arrays),
            out_specs=VMEM,
            out_shape=out,
            compiler_params=room(out),
        )(*arrays)

    one, two = steps
    side, turn, both = (one, two), (two, one), (one ^ two, one ^ two)
    near, across = 1, n.n_z - 1
    z1, z3 = over_z(bulk, near), over_z(bulk, across)
    z2 = over_z(z1, across)
    early = [bulk, over_pair(bulk, 0), over_pair(bulk, 1)]
    early.append(over_pair(early[1], 1))
    early, z1, z3 = lax.optimization_barrier((early, z1, z3))
    outer = join(z1, z3)
    trip = [over_pair(outer, 0), over_pair(outer, 1), over_pair(z2, 0), over_pair(z2, 1)]
    trip = lax.optimization_barrier(trip)
    low = (n.bulk // 2 + 7) // 8 * 8
    out = [shape(n.bulk + low, LANES), shape(2 * n.bulk - low, LANES)]
    ends = pl.pallas_call(
        functools.partial(cut_kernel, n, low),
        in_specs=[VMEM] * 4,
        out_specs=[VMEM] * 2,
        out_shape=out,
        compiler_params=room(*out),
    )(*trip)
    last = join(over_pair(ends[0], 1), over_pair(ends[1], 0))
    part = [join(*early, outer, z2)]
    part.append(join(*trip))
    here = (0, 0)
    shell, beyond = (near, across), (near ^ across,)
    pieces = [(here, (0,)), (side, (0,)), (turn, (0,)), (both, (0,)), (here, shell), (here, beyond)]
    pieces = [pieces, [(side, shell), (turn, shell), (side, beyond), (turn, beyond)]]
    store = [
        shape(n.total * n.slots, LANES),
        shape(n.nodes // CORES, n.total, LANES),
        shape(n.n_row, n.n_col * n.rows_c, LANES),
        shape(n.n_row, n.n_col, 8, LANES),
    ]
    taken = [*part, *[over_core(p) for p in part]]
    placed = pl.pallas_call(
        functools.partial(fill_kernel, n, pieces),
        in_specs=[VMEM] * len(taken),
        out_specs=[VMEM] * 4,
        out_shape=store,
        compiler_params=room(*taken, *store),
    )(*taken)
    pieces = [(both, (near, near ^ across, across))]
    taken = [last, over_core(last), *placed, view(diag_inverse)]
    out = [shape(n.wide * n.nodes, LANES), shape(n.wide * n.slots, LANES), *store]
    columns, schur, *_ = pl.pallas_call(
        functools.partial(work_kernel, n, pieces),
        in_specs=[VMEM] * len(taken),
        out_specs=[VMEM] * len(out),
        out_shape=out,
        input_output_aliases={2 + i: 2 + i for i in range(4)},
        compiler_params=room(*taken, *out),
    )(*taken)
    schur = jnp.transpose(schur.reshape(n.wide, n.tiles, n.nodes, LANES), (0, 2, 1, 3))
    return columns.reshape(n.wide, n.nodes, LANES), schur.reshape(n.wide, n.nodes, n.width)


def local(inv_known, pattern, factor, listed, diag_inverse):
    n = Sizes(inv_known, pattern, factor, diag_inverse)
    plan = functools.partial(fast, n) if n.fits() else general
    return plan(inv_known, pattern, factor, listed, diag_inverse)


def solution(mesh):
    in_specs = (
        P("row", "col"),
        P("row", "col"),
        P(("row", "col"), None, None),
        P(("row", "col"), None),
        P("col", None, None),
    )
    out_specs = (P("col", None, "row"), P("col", None, None))
    return jax.shard_map(local, mesh=mesh, in_specs=in_specs, out_specs=out_specs, check_vma=False)
```

```python
import functools
import math

import jax
import jax.numpy as jnp
from jax import lax
from jax.experimental import pallas as pl
from jax.experimental.pallas import tpu as pltpu
from jax.sharding import PartitionSpec as P

LANES = 128
CORES = 2
AXES = ("row", "col")
VMEM = pl.BlockSpec(memory_space=pltpu.VMEM)


def room(*arrays):
    return pltpu.CompilerParams(vmem_limit_bytes=8 * sum(math.prod(a.shape) for a in arrays) + (1 << 20))


def exact(a, b, contract):
    return lax.dot_general(
        a, b, (contract, ((), ())), precision=lax.Precision.HIGHEST, preferred_element_type=jnp.float32
    )


def halves(x):
    high = x.astype(jnp.bfloat16)
    return high, (x - high.astype(jnp.float32)).astype(jnp.bfloat16)


def product(a, high, low):
    def dot(x, y):
        return lax.dot_general(x, y, (((1,), (0,)), ((), ())), preferred_element_type=jnp.float32)

    a_high, a_low = halves(a)
    return dot(a_high, high) + (dot(a_high, low) + dot(a_low, high))


def supernode_pass(present, masked, listed_f, diag_part, ratio):
    row_block, row_listed = (
        lax.all_gather(masked, "col", axis=0, tiled=True),
        lax.all_gather(listed_f, "col", axis=0, tiled=True),
    )
    held = lax.psum_scatter(
        jnp.einsum("ij,ika->jka", present, row_block, precision=lax.Precision.HIGHEST),
        "row",
        scatter_dimension=0,
        tiled=True,
    )
    count_row = lax.axis_size("row")
    count_col = lax.axis_size("col")
    local_rows = held.shape[0]
    nodes = held.shape[1]
    narrow = held.shape[2] // count_col
    by_column = lax.all_to_all(held[None], "col", split_axis=3, concat_axis=0, tiled=True)
    grouped = by_column.reshape(count_row, 1, ratio, local_rows, nodes, narrow)
    moved = lax.all_to_all(grouped, "row", split_axis=0, concat_axis=1, tiled=True)
    ordered = jnp.transpose(moved[0], (1, 0, 2, 3, 4)).reshape(
        ratio * count_row * local_rows, nodes, narrow
    )
    summed = jnp.transpose(ordered, (2, 1, 0))
    columns = -summed * jnp.transpose(row_listed)[None, :, :]
    update = jnp.einsum("akj,jkb->akb", columns, row_block, precision=lax.Precision.HIGHEST)
    schur = diag_part - lax.psum(update, "row")
    return (columns, schur)


def general(inv_known, pattern, factor, listed, diag_inverse):
    tile = inv_known.shape[0] // pattern.shape[0]
    flags = pattern.astype(jnp.float32)
    spread = jnp.repeat(jnp.repeat(flags, tile, axis=0), tile, axis=1)
    present = inv_known * spread
    listed_f = listed.astype(jnp.float32)
    masked = factor * listed_f[:, :, None]
    ratio = lax.axis_size("col") // lax.axis_size("row")
    return supernode_pass(present, masked, listed_f, diag_inverse, ratio)


class Sizes:
    def __init__(self, inv_known, pattern, factor, diag_inverse):
        self.n_row = lax.axis_size("row")
        self.n_col = lax.axis_size("col")
        self.n_z = self.n_col // CORES
        self.own = factor.shape[0]
        self.nodes = factor.shape[1]
        self.width = factor.shape[2]
        self.tiles = self.width // LANES
        self.slots = self.tiles * self.nodes
        self.rows_r = inv_known.shape[0]
        self.rows_c = inv_known.shape[1]
        self.wide = diag_inverse.shape[0]
        self.pattern = pattern.shape
        self.span = self.n_col * self.own
        self.m_rows = self.own * self.slots
        self.bulk = self.m_rows + self.rows_c + 8
        self.total = self.n_row * self.rows_r

    def fits(self):
        return (
            self.n_col % CORES == 0
            and self.n_row == 2 * CORES
            and self.n_z == 2 * CORES
            and self.wide * CORES == LANES
            and self.rows_r == LANES
            and self.span == LANES
            and self.width % LANES == 0
            and self.slots % 8 == 0
            and self.own % 16 == 0
            and self.rows_c % 16 == 0
            and self.nodes % CORES == 0
            and self.nodes <= 8
        )


def spot():
    r = lax.axis_index("row")
    c = lax.axis_index("col")
    return r, lax.div(c, CORES), lax.rem(c, CORES)


def pack_kernel(n, factor_h, listed_h, inv_h, pattern_h, bulk, factor, listed_t, inv_t, pattern_t, wide_l, sems):
    pairs = ((factor_h, factor), (listed_h, listed_t), (inv_h, inv_t), (pattern_h, pattern_t))
    copies = [pltpu.make_async_copy(a, b, sems.at[i]) for i, (a, b) in enumerate(pairs)]
    for copy in copies:
        copy.start()
    for copy in copies:
        copy.wait()
    _, z, core = spot()
    col = z * CORES + core
    wide_l[...] = jnp.zeros((8, LANES), jnp.float32)
    wide_l[pl.ds(0, n.nodes), pl.ds(0, n.own)] = listed_t[...].astype(jnp.float32)
    flags = wide_l[...]
    row = lax.broadcasted_iota(jnp.int32, (n.m_rows, LANES), 0)
    lane = lax.broadcasted_iota(jnp.int32, (n.m_rows, LANES), 1)
    node = lax.rem(row, n.nodes)
    mine = jnp.zeros((n.m_rows, LANES), jnp.float32)
    for k in range(n.nodes):
        mine = jnp.where(node == k, flags[k : k + 1, :], mine)
    keep = jnp.sum(jnp.where(lane == lax.div(row, n.slots), mine, 0.0), axis=1, keepdims=True)
    bulk[pl.ds(0, n.m_rows), :] = factor[...] * keep
    bulk[pl.ds(n.m_rows + n.rows_c, 8), :] = pltpu.roll(flags, col * n.own, 1)
    high = n.rows_r // n.pattern[0]
    deep = n.rows_c // n.pattern[1]
    tile = lax.div(lax.broadcasted_iota(jnp.int32, (1, LANES), 1), high)
    for q in range(n.pattern[1]):
        keep = jnp.zeros((1, LANES), jnp.float32)
        for p in range(n.pattern[0]):
            keep = jnp.where(tile == p, pattern_t[q : q + 1, p : p + 1].astype(jnp.float32), keep)
        bulk[pl.ds(n.m_rows + q * deep, deep), :] = inv_t[pl.ds(q * deep, deep), :] * keep


def join_kernel(n, *refs):
    out = refs[-1]
    at = 0
    for ref in refs[:-1]:
        out[pl.ds(at, ref.shape[0]), :] = ref[...]
        at += ref.shape[0]


def cut_kernel(n, low, f_outer, s_outer, f_far, s_far, one, two):
    one[pl.ds(0, n.bulk), :] = f_outer[pl.ds(0, n.bulk), :]
    one[pl.ds(n.bulk, low), :] = f_far[pl.ds(0, low), :]
    two[pl.ds(0, n.bulk - low), :] = s_far[pl.ds(low, n.bulk - low), :]
    two[pl.ds(n.bulk - low, n.bulk), :] = s_outer[pl.ds(n.bulk, n.bulk), :]


def put(n, ref, at, r2, c2, m_high, m_low, m_sel, p_high, p_low, mask):
    _, z, core = spot()
    first = core == 0
    left = lax.broadcasted_iota(jnp.int32, (n.own, LANES), 1) < n.wide
    rows = pl.ds(pl.multiple_of(r2 * n.span + c2 * n.own, n.own), n.own)
    cols = pl.ds(pl.multiple_of(c2 * n.rows_c, n.rows_c), n.rows_c)
    p_high[r2, cols, :], p_low[r2, cols, :] = halves(ref[pl.ds(at + n.m_rows, n.rows_c), :])
    mask[r2, c2] = ref[pl.ds(at + n.m_rows + n.rows_c, 8), :]
    chosen = []
    for k in range(n.nodes):
        piece = None
        for t in range(n.tiles):
            load = ref[pl.ds(at + t * n.nodes + k, n.own, stride=n.slots), :]
            lanes = pl.ds(t * LANES, LANES)
            m_high[k, rows, lanes], m_low[k, rows, lanes] = halves(load)
            piece = load if piece is None else jnp.where(z == t, load, piece)
        chosen.append(piece)
    for k in range(0, n.nodes, CORES):
        one, two = chosen[k], chosen[k + 1]
        turned = pltpu.roll(jnp.where(first, two, one), n.wide, 1)
        m_sel[k // CORES, rows, :] = jnp.where(left == first, jnp.where(first, one, two), turned)


def fill(n, pieces, mine, theirs, *refs):
    r, z, core = spot()
    for ref, owner in ((mine, core), (theirs, core ^ 1)):
        at = 0
        for shift, shells in pieces:
            for s in shells:
                put(n, ref, at, r ^ choose(owner, shift), (z ^ s) * CORES + owner, *refs)
                at += n.bulk


def fill_kernel(n, pieces, *refs):
    count = len(pieces)
    for i, group in enumerate(pieces):
        fill(n, group, refs[i], refs[count + i], *refs[2 * count :])


def work_kernel(n, pieces, mine, theirs, *refs):
    diag, columns, schur, *store = refs[6:]
    fill(n, pieces, mine, theirs, *store)
    m_high, m_low, m_sel, p_high, p_low, masks = store
    r, _, _ = spot()
    mask = []
    for i in range(n.n_row):
        total = masks[i, 0]
        for c in range(1, n.n_col):
            total += masks[i, c]
        mask.append(total)
    p_all = [jnp.concatenate([p[i] for i in range(n.n_row)], axis=1) for p in (p_high, p_low)]
    for k in range(n.nodes):
        if k % CORES == 0:
            x_t = product(m_sel[k // CORES].T, *p_all)
        at = k % CORES * n.wide
        spread = jnp.concatenate([m[k : k + 1, :] for m in mask], axis=1)
        part = -x_t[at : at + n.wide, :] * spread
        own = part[:, :LANES]
        for i in range(1, n.n_row):
            own = jnp.where(r == i, part[:, i * LANES : (i + 1) * LANES], own)
        columns[pl.ds(k, n.wide, stride=n.nodes), :] = own
        wide = product(part, m_high[k], m_low[k])
        for t in range(n.tiles):
            line = pl.ds(t * n.nodes + k, n.wide, stride=n.slots)
            schur[line, :] = diag[line, :] - wide[:, t * LANES : (t + 1) * LANES]


def choose(core, pair):
    return jnp.where(core == 0, pair[0], pair[1])


def fast(n, inv_known, pattern, factor, listed, diag_inverse):
    def shape(*dims):
        return jax.ShapeDtypeStruct(dims, jnp.float32)

    def route(array, change):
        pairs = []
        for r in range(n.n_row):
            for z in range(n.n_z):
                for core in range(CORES):
                    r2, z2, core2 = change(r, z, core)
                    pairs.append(((r * n.n_z + z) * CORES + core, (r2 * n.n_z + z2) * CORES + core2))
        return lax.ppermute(array, AXES, pairs)

    def over_z(array, s):
        return route(array, lambda r, z, core: (r, z ^ s, core))

    def over_core(array):
        return route(array, lambda r, z, core: (r, z, core ^ 1))

    steps = [1 << i for i in range(n.n_row.bit_length() - 1)]

    def over_pair(array, i):
        return route(array, lambda r, z, core: (r ^ (steps[i] if core == 0 else steps[-1 - i]), z, core))

    def view(array):
        lead = array.shape[0]
        split = array.reshape(lead, n.nodes, n.tiles, LANES)
        return jnp.transpose(split, (0, 2, 1, 3)).reshape(lead * n.slots, LANES)

    taken = [pltpu.with_memory_space_constraint(a, pltpu.HBM) for a in (view(factor), listed.T, inv_known.T, pattern.T)]
    out = shape(n.bulk, LANES)
    bulk = pl.pallas_call(
        functools.partial(pack_kernel, n),
        in_specs=[pl.BlockSpec(memory_space=pltpu.HBM)] * 4,
        out_specs=VMEM,
        out_shape=out,
        scratch_shapes=[pltpu.VMEM(a.shape, a.dtype) for a in taken]
        + [pltpu.VMEM((8, LANES), jnp.float32), pltpu.SemaphoreType.DMA((len(taken),))],
        compiler_params=room(out, *taken),
    )(*taken)

    def join(*arrays):
        out = shape(sum(a.shape[0] for a in arrays), LANES)
        return pl.pallas_call(
            functools.partial(join_kernel, n),
            in_specs=[VMEM] * len(arrays),
            out_specs=VMEM,
            out_shape=out,
            compiler_params=room(out),
        )(*arrays)

    one, two = steps
    side, turn, both = (one, two), (two, one), (one ^ two, one ^ two)
    near, across = 1, n.n_z - 1
    z1, z3 = over_z(bulk, near), over_z(bulk, across)
    z2 = over_z(z1, across)
    mid, z1 = lax.optimization_barrier((bulk, z1))
    early = [bulk, over_pair(mid, 0), over_pair(mid, 1)]
    early.append(over_pair(early[1], 1))
    outer = join(z1, z3)
    trip = [over_pair(outer, 0), over_pair(outer, 1), over_pair(z2, 0), over_pair(z2, 1)]
    trip = lax.optimization_barrier(trip)
    low = (n.bulk // 2 + 7) // 8 * 8
    out = [shape(n.bulk + low, LANES), shape(2 * n.bulk - low, LANES)]
    ends = pl.pallas_call(
        functools.partial(cut_kernel, n, low),
        in_specs=[VMEM] * 4,
        out_specs=[VMEM] * 2,
        out_shape=out,
        compiler_params=room(*out),
    )(*trip)
    last = join(over_pair(ends[0], 1), over_pair(ends[1], 0))
    part = [join(*early, outer, z2)]
    part.append(join(*trip))
    here = (0, 0)
    shell, beyond = (near, across), (near ^ across,)
    pieces = [(here, (0,)), (side, (0,)), (turn, (0,)), (both, (0,)), (here, shell), (here, beyond)]
    pieces = [pieces, [(side, shell), (turn, shell), (side, beyond), (turn, beyond)]]
    def short(*dims):
        return [jax.ShapeDtypeStruct(dims, jnp.bfloat16)] * 2

    store = [
        *short(n.nodes, n.total, n.width),
        shape(n.nodes // CORES, n.total, LANES),
        *short(n.n_row, n.n_col * n.rows_c, LANES),
        shape(n.n_row, n.n_col, 8, LANES),
    ]
    taken = [*part, *[over_core(p) for p in part]]
    placed = pl.pallas_call(
        functools.partial(fill_kernel, n, pieces),
        in_specs=[VMEM] * len(taken),
        out_specs=[VMEM] * len(store),
        out_shape=store,
        compiler_params=room(*taken, *store),
    )(*taken)
    pieces = [(both, (near, near ^ across, across))]
    taken = [last, over_core(last), *placed, view(diag_inverse)]
    out = [shape(n.wide * n.nodes, LANES), shape(n.wide * n.slots, LANES), *store]
    columns, schur, *_ = pl.pallas_call(
        functools.partial(work_kernel, n, pieces),
        in_specs=[VMEM] * len(taken),
        out_specs=[VMEM] * len(out),
        out_shape=out,
        input_output_aliases={2 + i: 2 + i for i in range(len(store))},
        compiler_params=room(*taken, *out),
    )(*taken)
    schur = jnp.transpose(schur.reshape(n.wide, n.tiles, n.nodes, LANES), (0, 2, 1, 3))
    return columns.reshape(n.wide, n.nodes, LANES), schur.reshape(n.wide, n.nodes, n.width)


def local(inv_known, pattern, factor, listed, diag_inverse):
    n = Sizes(inv_known, pattern, factor, diag_inverse)
    plan = functools.partial(fast, n) if n.fits() else general
    return plan(inv_known, pattern, factor, listed, diag_inverse)


def solution(mesh):
    in_specs = (
        P("row", "col"),
        P("row", "col"),
        P(("row", "col"), None, None),
        P(("row", "col"), None),
        P("col", None, None),
    )
    out_specs = (P("col", None, "row"), P("col", None, None))
    return jax.shard_map(local, mesh=mesh, in_specs=in_specs, out_specs=out_specs, check_vma=False)
```

```python
import functools
import math

import jax
import jax.numpy as jnp
from jax import lax
from jax.experimental import pallas as pl
from jax.experimental.pallas import tpu as pltpu
from jax.sharding import PartitionSpec as P

LANES = 128
CORES = 2
AXES = ("row", "col")
VMEM = pl.BlockSpec(memory_space=pltpu.VMEM)


def room(*arrays):
    return pltpu.CompilerParams(vmem_limit_bytes=8 * sum(math.prod(a.shape) for a in arrays) + (1 << 20))


def exact(a, b, contract):
    return lax.dot_general(
        a, b, (contract, ((), ())), precision=lax.Precision.HIGHEST, preferred_element_type=jnp.float32
    )


def halves(x):
    high = x.astype(jnp.bfloat16)
    return high, (x - high.astype(jnp.float32)).astype(jnp.bfloat16)


def product(a, high, low):
    def dot(x, y):
        return lax.dot_general(x, y, (((1,), (0,)), ((), ())), preferred_element_type=jnp.float32)

    a_high, a_low = halves(a)
    return dot(a_high, high) + (dot(a_high, low) + dot(a_low, high))


def supernode_pass(present, masked, listed_f, diag_part, ratio):
    row_block, row_listed = (
        lax.all_gather(masked, "col", axis=0, tiled=True),
        lax.all_gather(listed_f, "col", axis=0, tiled=True),
    )
    held = lax.psum_scatter(
        jnp.einsum("ij,ika->jka", present, row_block, precision=lax.Precision.HIGHEST),
        "row",
        scatter_dimension=0,
        tiled=True,
    )
    count_row = lax.axis_size("row")
    count_col = lax.axis_size("col")
    local_rows = held.shape[0]
    nodes = held.shape[1]
    narrow = held.shape[2] // count_col
    by_column = lax.all_to_all(held[None], "col", split_axis=3, concat_axis=0, tiled=True)
    grouped = by_column.reshape(count_row, 1, ratio, local_rows, nodes, narrow)
    moved = lax.all_to_all(grouped, "row", split_axis=0, concat_axis=1, tiled=True)
    ordered = jnp.transpose(moved[0], (1, 0, 2, 3, 4)).reshape(
        ratio * count_row * local_rows, nodes, narrow
    )
    summed = jnp.transpose(ordered, (2, 1, 0))
    columns = -summed * jnp.transpose(row_listed)[None, :, :]
    update = jnp.einsum("akj,jkb->akb", columns, row_block, precision=lax.Precision.HIGHEST)
    schur = diag_part - lax.psum(update, "row")
    return (columns, schur)


def general(inv_known, pattern, factor, listed, diag_inverse):
    tile = inv_known.shape[0] // pattern.shape[0]
    flags = pattern.astype(jnp.float32)
    spread = jnp.repeat(jnp.repeat(flags, tile, axis=0), tile, axis=1)
    present = inv_known * spread
    listed_f = listed.astype(jnp.float32)
    masked = factor * listed_f[:, :, None]
    ratio = lax.axis_size("col") // lax.axis_size("row")
    return supernode_pass(present, masked, listed_f, diag_inverse, ratio)


class Sizes:
    def __init__(self, inv_known, pattern, factor, diag_inverse):
        self.n_row = lax.axis_size("row")
        self.n_col = lax.axis_size("col")
        self.n_z = self.n_col // CORES
        self.own = factor.shape[0]
        self.nodes = factor.shape[1]
        self.width = factor.shape[2]
        self.tiles = self.width // LANES
        self.slots = self.tiles * self.nodes
        self.rows_r = inv_known.shape[0]
        self.rows_c = inv_known.shape[1]
        self.wide = diag_inverse.shape[0]
        self.pattern = pattern.shape
        self.span = self.n_col * self.own
        self.m_rows = self.own * self.slots
        self.bulk = self.m_rows + self.rows_c + 8
        self.total = self.n_row * self.rows_r

    def fits(self):
        return (
            self.n_col % CORES == 0
            and self.n_row == 2 * CORES
            and self.n_z == 2 * CORES
            and self.wide * CORES == LANES
            and self.rows_r == LANES
            and self.span == LANES
            and self.width % LANES == 0
            and self.slots % 8 == 0
            and self.own % 16 == 0
            and self.rows_c % 16 == 0
            and self.nodes % CORES == 0
            and self.nodes <= 8
        )


def spot():
    r = lax.axis_index("row")
    c = lax.axis_index("col")
    return r, lax.div(c, CORES), lax.rem(c, CORES)


def pack_kernel(n, factor_h, listed_h, inv_h, pattern_h, bulk, factor, listed_t, inv_t, pattern_t, wide_l, sems):
    pairs = ((factor_h, factor), (listed_h, listed_t), (inv_h, inv_t), (pattern_h, pattern_t))
    copies = [pltpu.make_async_copy(a, b, sems.at[i]) for i, (a, b) in enumerate(pairs)]
    for copy in copies:
        copy.start()
    for copy in copies:
        copy.wait()
    _, z, core = spot()
    col = z * CORES + core
    wide_l[...] = jnp.zeros((8, LANES), jnp.float32)
    wide_l[pl.ds(0, n.nodes), pl.ds(0, n.own)] = listed_t[...].astype(jnp.float32)
    flags = wide_l[...]
    row = lax.broadcasted_iota(jnp.int32, (n.m_rows, LANES), 0)
    lane = lax.broadcasted_iota(jnp.int32, (n.m_rows, LANES), 1)
    node = lax.rem(row, n.nodes)
    mine = jnp.zeros((n.m_rows, LANES), jnp.float32)
    for k in range(n.nodes):
        mine = jnp.where(node == k, flags[k : k + 1, :], mine)
    keep = jnp.sum(jnp.where(lane == lax.div(row, n.slots), mine, 0.0), axis=1, keepdims=True)
    bulk[pl.ds(0, n.m_rows), :] = factor[...] * keep
    bulk[pl.ds(n.m_rows + n.rows_c, 8), :] = pltpu.roll(flags, col * n.own, 1)
    high = n.rows_r // n.pattern[0]
    deep = n.rows_c // n.pattern[1]
    tile = lax.div(lax.broadcasted_iota(jnp.int32, (1, LANES), 1), high)
    for q in range(n.pattern[1]):
        keep = jnp.zeros((1, LANES), jnp.float32)
        for p in range(n.pattern[0]):
            keep = jnp.where(tile == p, pattern_t[q : q + 1, p : p + 1].astype(jnp.float32), keep)
        bulk[pl.ds(n.m_rows + q * deep, deep), :] = inv_t[pl.ds(q * deep, deep), :] * keep


def join_kernel(n, *refs):
    out = refs[-1]
    at = 0
    for ref in refs[:-1]:
        out[pl.ds(at, ref.shape[0]), :] = ref[...]
        at += ref.shape[0]


def cut_kernel(n, low, f_outer, s_outer, f_far, s_far, one, two):
    one[pl.ds(0, n.bulk), :] = f_outer[pl.ds(0, n.bulk), :]
    one[pl.ds(n.bulk, low), :] = f_far[pl.ds(0, low), :]
    two[pl.ds(0, n.bulk - low), :] = s_far[pl.ds(low, n.bulk - low), :]
    two[pl.ds(n.bulk - low, n.bulk), :] = s_outer[pl.ds(n.bulk, n.bulk), :]


def put(n, ref, at, r2, c2, m_high, m_low, m_sel, p_high, p_low, mask):
    _, z, core = spot()
    first = core == 0
    left = lax.broadcasted_iota(jnp.int32, (n.own, LANES), 1) < n.wide
    rows = pl.ds(pl.multiple_of(r2 * n.span + c2 * n.own, n.own), n.own)
    cols = pl.ds(pl.multiple_of(c2 * n.rows_c, n.rows_c), n.rows_c)
    p_high[r2, cols, :], p_low[r2, cols, :] = halves(ref[pl.ds(at + n.m_rows, n.rows_c), :])
    mask[r2, c2] = ref[pl.ds(at + n.m_rows + n.rows_c, 8), :]
    chosen = []
    for k in range(n.nodes):
        piece = None
        for t in range(n.tiles):
            load = ref[pl.ds(at + t * n.nodes + k, n.own, stride=n.slots), :]
            lanes = pl.ds(t * LANES, LANES)
            m_high[k, rows, lanes], m_low[k, rows, lanes] = halves(load)
            piece = load if piece is None else jnp.where(z == t, load, piece)
        chosen.append(piece)
    for k in range(0, n.nodes, CORES):
        one, two = chosen[k], chosen[k + 1]
        turned = pltpu.roll(jnp.where(first, two, one), n.wide, 1)
        m_sel[k // CORES, rows, :] = jnp.where(left == first, jnp.where(first, one, two), turned)


def fill(n, pieces, mine, theirs, *refs):
    r, z, core = spot()
    for ref, owner in ((mine, core), (theirs, core ^ 1)):
        at = 0
        for shift, shells in pieces:
            for s in shells:
                put(n, ref, at, r ^ choose(owner, shift), (z ^ s) * CORES + owner, *refs)
                at += n.bulk


def fill_kernel(n, pieces, *refs):
    count = len(pieces)
    for i, group in enumerate(pieces):
        fill(n, group, refs[i], refs[count + i], *refs[2 * count :])


def work_kernel(n, pieces, mine, theirs, *refs):
    diag, columns, schur, *store = refs[6:]
    fill(n, pieces, mine, theirs, *store)
    m_high, m_low, m_sel, p_high, p_low, masks = store
    r, _, _ = spot()
    mask = []
    for i in range(n.n_row):
        total = masks[i, 0]
        for c in range(1, n.n_col):
            total += masks[i, c]
        mask.append(total)
    p_all = [jnp.concatenate([p[i] for i in range(n.n_row)], axis=1) for p in (p_high, p_low)]
    for k in range(n.nodes):
        if k % CORES == 0:
            x_t = product(m_sel[k // CORES].T, *p_all)
        at = k % CORES * n.wide
        spread = jnp.concatenate([m[k : k + 1, :] for m in mask], axis=1)
        part = -x_t[at : at + n.wide, :] * spread
        own = part[:, :LANES]
        for i in range(1, n.n_row):
            own = jnp.where(r == i, part[:, i * LANES : (i + 1) * LANES], own)
        columns[pl.ds(k, n.wide, stride=n.nodes), :] = own
        wide = product(part, m_high[k], m_low[k])
        for t in range(n.tiles):
            line = pl.ds(t * n.nodes + k, n.wide, stride=n.slots)
            schur[line, :] = diag[line, :] - wide[:, t * LANES : (t + 1) * LANES]


def choose(core, pair):
    return jnp.where(core == 0, pair[0], pair[1])


def fast(n, inv_known, pattern, factor, listed, diag_inverse):
    def shape(*dims):
        return jax.ShapeDtypeStruct(dims, jnp.float32)

    def route(array, change):
        pairs = []
        for r in range(n.n_row):
            for z in range(n.n_z):
                for core in range(CORES):
                    r2, z2, core2 = change(r, z, core)
                    pairs.append(((r * n.n_z + z) * CORES + core, (r2 * n.n_z + z2) * CORES + core2))
        return lax.ppermute(array, AXES, pairs)

    def over_z(array, s):
        return route(array, lambda r, z, core: (r, z ^ s, core))

    def over_core(array):
        return route(array, lambda r, z, core: (r, z, core ^ 1))

    steps = [1 << i for i in range(n.n_row.bit_length() - 1)]

    def over_pair(array, i):
        return route(array, lambda r, z, core: (r ^ (steps[i] if core == 0 else steps[-1 - i]), z, core))

    def view(array):
        lead = array.shape[0]
        split = array.reshape(lead, n.nodes, n.tiles, LANES)
        return jnp.transpose(split, (0, 2, 1, 3)).reshape(lead * n.slots, LANES)

    taken = [pltpu.with_memory_space_constraint(a, pltpu.HBM) for a in (view(factor), listed.T, inv_known.T, pattern.T)]
    out = shape(n.bulk, LANES)
    bulk = pl.pallas_call(
        functools.partial(pack_kernel, n),
        in_specs=[pl.BlockSpec(memory_space=pltpu.HBM)] * 4,
        out_specs=VMEM,
        out_shape=out,
        scratch_shapes=[pltpu.VMEM(a.shape, a.dtype) for a in taken]
        + [pltpu.VMEM((8, LANES), jnp.float32), pltpu.SemaphoreType.DMA((len(taken),))],
        compiler_params=room(out, *taken),
    )(*taken)

    def join(*arrays):
        out = shape(sum(a.shape[0] for a in arrays), LANES)
        return pl.pallas_call(
            functools.partial(join_kernel, n),
            in_specs=[VMEM] * len(arrays),
            out_specs=VMEM,
            out_shape=out,
            compiler_params=room(out),
        )(*arrays)

    one, two = steps
    side, turn, both = (one, two), (two, one), (one ^ two, one ^ two)
    near, across = 1, n.n_z - 1
    z1, z3 = over_z(bulk, near), over_z(bulk, across)
    z2 = over_z(z3, near)
    mid, z1 = lax.optimization_barrier((bulk, z1))
    early = [bulk, over_pair(mid, 0), over_pair(mid, 1)]
    early.append(over_pair(early[1], 1))
    outer = join(z1, z3)
    trip = [over_pair(outer, 0), over_pair(outer, 1), over_pair(z2, 0), over_pair(z2, 1)]
    trip = lax.optimization_barrier(trip)
    low = (n.bulk // 2 + 7) // 8 * 8
    out = [shape(n.bulk + low, LANES), shape(2 * n.bulk - low, LANES)]
    ends = pl.pallas_call(
        functools.partial(cut_kernel, n, low),
        in_specs=[VMEM] * 4,
        out_specs=[VMEM] * 2,
        out_shape=out,
        compiler_params=room(*out),
    )(*trip)
    last = join(over_pair(ends[0], 1), over_pair(ends[1], 0))
    part = [join(*early, outer, z2)]
    part.append(join(*trip))
    here = (0, 0)
    shell, beyond = (near, across), (near ^ across,)
    pieces = [(here, (0,)), (side, (0,)), (turn, (0,)), (both, (0,)), (here, shell), (here, beyond)]
    pieces = [pieces, [(side, shell), (turn, shell), (side, beyond), (turn, beyond)]]
    def short(*dims):
        return [jax.ShapeDtypeStruct(dims, jnp.bfloat16)] * 2

    store = [
        *short(n.nodes, n.total, n.width),
        shape(n.nodes // CORES, n.total, LANES),
        *short(n.n_row, n.n_col * n.rows_c, LANES),
        shape(n.n_row, n.n_col, 8, LANES),
    ]
    taken = [*part, *[over_core(p) for p in part]]
    placed = pl.pallas_call(
        functools.partial(fill_kernel, n, pieces),
        in_specs=[VMEM] * len(taken),
        out_specs=[VMEM] * len(store),
        out_shape=store,
        compiler_params=room(*taken, *store),
    )(*taken)
    pieces = [(both, (near, near ^ across, across))]
    taken = [last, over_core(last), *placed, view(diag_inverse)]
    out = [shape(n.wide * n.nodes, LANES), shape(n.wide * n.slots, LANES), *store]
    columns, schur, *_ = pl.pallas_call(
        functools.partial(work_kernel, n, pieces),
        in_specs=[VMEM] * len(taken),
        out_specs=[VMEM] * len(out),
        out_shape=out,
        input_output_aliases={2 + i: 2 + i for i in range(len(store))},
        compiler_params=room(*taken, *out),
    )(*taken)
    schur = jnp.transpose(schur.reshape(n.wide, n.tiles, n.nodes, LANES), (0, 2, 1, 3))
    return columns.reshape(n.wide, n.nodes, LANES), schur.reshape(n.wide, n.nodes, n.width)


def local(inv_known, pattern, factor, listed, diag_inverse):
    n = Sizes(inv_known, pattern, factor, diag_inverse)
    plan = functools.partial(fast, n) if n.fits() else general
    return plan(inv_known, pattern, factor, listed, diag_inverse)


def solution(mesh):
    in_specs = (
        P("row", "col"),
        P("row", "col"),
        P(("row", "col"), None, None),
        P(("row", "col"), None),
        P("col", None, None),
    )
    out_specs = (P("col", None, "row"), P("col", None, None))
    return jax.shard_map(local, mesh=mesh, in_specs=in_specs, out_specs=out_specs, check_vma=False)
```

```python
import functools
import math

import jax
import jax.numpy as jnp
from jax import lax
from jax.experimental import pallas as pl
from jax.experimental.pallas import tpu as pltpu
from jax.sharding import PartitionSpec as P

LANES = 128
CORES = 2
AXES = ("row", "col")
VMEM = pl.BlockSpec(memory_space=pltpu.VMEM)


def room(*arrays):
    return pltpu.CompilerParams(vmem_limit_bytes=8 * sum(math.prod(a.shape) for a in arrays) + (1 << 20))


def exact(a, b, contract):
    return lax.dot_general(
        a, b, (contract, ((), ())), precision=lax.Precision.HIGHEST, preferred_element_type=jnp.float32
    )


def halves(x):
    high = x.astype(jnp.bfloat16)
    return high, (x - high.astype(jnp.float32)).astype(jnp.bfloat16)


def product(a, high, low):
    def dot(x, y):
        return lax.dot_general(x, y, (((1,), (0,)), ((), ())), preferred_element_type=jnp.float32)

    a_high, a_low = halves(a)
    return dot(a_high, high) + (dot(a_high, low) + dot(a_low, high))


def supernode_pass(present, masked, listed_f, diag_part, ratio):
    row_block, row_listed = (
        lax.all_gather(masked, "col", axis=0, tiled=True),
        lax.all_gather(listed_f, "col", axis=0, tiled=True),
    )
    held = lax.psum_scatter(
        jnp.einsum("ij,ika->jka", present, row_block, precision=lax.Precision.HIGHEST),
        "row",
        scatter_dimension=0,
        tiled=True,
    )
    count_row = lax.axis_size("row")
    count_col = lax.axis_size("col")
    local_rows = held.shape[0]
    nodes = held.shape[1]
    narrow = held.shape[2] // count_col
    by_column = lax.all_to_all(held[None], "col", split_axis=3, concat_axis=0, tiled=True)
    grouped = by_column.reshape(count_row, 1, ratio, local_rows, nodes, narrow)
    moved = lax.all_to_all(grouped, "row", split_axis=0, concat_axis=1, tiled=True)
    ordered = jnp.transpose(moved[0], (1, 0, 2, 3, 4)).reshape(
        ratio * count_row * local_rows, nodes, narrow
    )
    summed = jnp.transpose(ordered, (2, 1, 0))
    columns = -summed * jnp.transpose(row_listed)[None, :, :]
    update = jnp.einsum("akj,jkb->akb", columns, row_block, precision=lax.Precision.HIGHEST)
    schur = diag_part - lax.psum(update, "row")
    return (columns, schur)


def general(inv_known, pattern, factor, listed, diag_inverse):
    tile = inv_known.shape[0] // pattern.shape[0]
    flags = pattern.astype(jnp.float32)
    spread = jnp.repeat(jnp.repeat(flags, tile, axis=0), tile, axis=1)
    present = inv_known * spread
    listed_f = listed.astype(jnp.float32)
    masked = factor * listed_f[:, :, None]
    ratio = lax.axis_size("col") // lax.axis_size("row")
    return supernode_pass(present, masked, listed_f, diag_inverse, ratio)


class Sizes:
    def __init__(self, inv_known, pattern, factor, diag_inverse):
        self.n_row = lax.axis_size("row")
        self.n_col = lax.axis_size("col")
        self.n_z = self.n_col // CORES
        self.own = factor.shape[0]
        self.nodes = factor.shape[1]
        self.width = factor.shape[2]
        self.tiles = self.width // LANES
        self.slots = self.tiles * self.nodes
        self.rows_r = inv_known.shape[0]
        self.rows_c = inv_known.shape[1]
        self.wide = diag_inverse.shape[0]
        self.pattern = pattern.shape
        self.span = self.n_col * self.own
        self.m_rows = self.own * self.slots
        self.bulk = self.m_rows + self.rows_c + 8
        self.total = self.n_row * self.rows_r

    def fits(self):
        return (
            self.n_col % CORES == 0
            and self.n_row == 2 * CORES
            and self.n_z == 2 * CORES
            and self.wide * CORES == LANES
            and self.rows_r == LANES
            and self.span == LANES
            and self.width % LANES == 0
            and self.slots % 8 == 0
            and self.own % 16 == 0
            and self.rows_c % 16 == 0
            and self.nodes % CORES == 0
            and self.nodes <= 8
        )


def spot():
    r = lax.axis_index("row")
    c = lax.axis_index("col")
    return r, lax.div(c, CORES), lax.rem(c, CORES)


def pack_kernel(n, factor_h, listed_h, inv_h, pattern_h, bulk, factor, listed_t, inv_t, pattern_t, wide_l, sems):
    pairs = ((factor_h, factor), (listed_h, listed_t), (inv_h, inv_t), (pattern_h, pattern_t))
    copies = [pltpu.make_async_copy(a, b, sems.at[i]) for i, (a, b) in enumerate(pairs)]
    for copy in copies:
        copy.start()
    for copy in copies:
        copy.wait()
    _, z, core = spot()
    col = z * CORES + core
    wide_l[...] = jnp.zeros((8, LANES), jnp.float32)
    wide_l[pl.ds(0, n.nodes), pl.ds(0, n.own)] = listed_t[...].astype(jnp.float32)
    flags = wide_l[...]
    row = lax.broadcasted_iota(jnp.int32, (n.m_rows, LANES), 0)
    lane = lax.broadcasted_iota(jnp.int32, (n.m_rows, LANES), 1)
    node = lax.rem(row, n.nodes)
    mine = jnp.zeros((n.m_rows, LANES), jnp.float32)
    for k in range(n.nodes):
        mine = jnp.where(node == k, flags[k : k + 1, :], mine)
    keep = jnp.sum(jnp.where(lane == lax.div(row, n.slots), mine, 0.0), axis=1, keepdims=True)
    bulk[pl.ds(0, n.m_rows), :] = factor[...] * keep
    bulk[pl.ds(n.m_rows + n.rows_c, 8), :] = pltpu.roll(flags, col * n.own, 1)
    high = n.rows_r // n.pattern[0]
    deep = n.rows_c // n.pattern[1]
    tile = lax.div(lax.broadcasted_iota(jnp.int32, (1, LANES), 1), high)
    for q in range(n.pattern[1]):
        keep = jnp.zeros((1, LANES), jnp.float32)
        for p in range(n.pattern[0]):
            keep = jnp.where(tile == p, pattern_t[q : q + 1, p : p + 1].astype(jnp.float32), keep)
        bulk[pl.ds(n.m_rows + q * deep, deep), :] = inv_t[pl.ds(q * deep, deep), :] * keep


def join_kernel(n, *refs):
    out = refs[-1]
    at = 0
    for ref in refs[:-1]:
        out[pl.ds(at, ref.shape[0]), :] = ref[...]
        at += ref.shape[0]


def cut_kernel(n, low, f_outer, s_outer, f_far, s_far, one, two):
    one[pl.ds(0, n.bulk), :] = f_outer[pl.ds(0, n.bulk), :]
    one[pl.ds(n.bulk, low), :] = f_far[pl.ds(0, low), :]
    two[pl.ds(0, n.bulk - low), :] = s_far[pl.ds(low, n.bulk - low), :]
    two[pl.ds(n.bulk - low, n.bulk), :] = s_outer[pl.ds(n.bulk, n.bulk), :]


def put(n, ref, at, r2, c2, m_high, m_low, m_sel, p_high, p_low, mask):
    _, z, core = spot()
    first = core == 0
    left = lax.broadcasted_iota(jnp.int32, (n.own, LANES), 1) < n.wide
    rows = pl.ds(pl.multiple_of(r2 * n.span + c2 * n.own, n.own), n.own)
    cols = pl.ds(pl.multiple_of(c2 * n.rows_c, n.rows_c), n.rows_c)
    p_high[r2, cols, :], p_low[r2, cols, :] = halves(ref[pl.ds(at + n.m_rows, n.rows_c), :])
    mask[r2, c2] = ref[pl.ds(at + n.m_rows + n.rows_c, 8), :]
    chosen = []
    for k in range(n.nodes):
        piece = None
        for t in range(n.tiles):
            load = ref[pl.ds(at + t * n.nodes + k, n.own, stride=n.slots), :]
            lanes = pl.ds(t * LANES, LANES)
            m_high[k, rows, lanes], m_low[k, rows, lanes] = halves(load)
            piece = load if piece is None else jnp.where(z == t, load, piece)
        chosen.append(piece)
    for k in range(0, n.nodes, CORES):
        one, two = chosen[k], chosen[k + 1]
        turned = pltpu.roll(jnp.where(first, two, one), n.wide, 1)
        m_sel[k // CORES, rows, :] = jnp.where(left == first, jnp.where(first, one, two), turned)


def fill(n, pieces, mine, theirs, *refs):
    r, z, core = spot()
    for ref, owner in ((mine, core), (theirs, core ^ 1)):
        at = 0
        for shift, shells in pieces:
            for s in shells:
                put(n, ref, at, r ^ choose(owner, shift), (z ^ s) * CORES + owner, *refs)
                at += n.bulk


def fill_kernel(n, pieces, *refs):
    count = len(pieces)
    for i, group in enumerate(pieces):
        fill(n, group, refs[i], refs[count + i], *refs[2 * count :])


def work_kernel(n, pieces, mine, theirs, *refs):
    diag, columns, schur, *store = refs[6:]
    fill(n, pieces, mine, theirs, *store)
    m_high, m_low, m_sel, p_high, p_low, masks = store
    r, _, _ = spot()
    mask = []
    for i in range(n.n_row):
        total = masks[i, 0]
        for c in range(1, n.n_col):
            total += masks[i, c]
        mask.append(total)
    p_all = [jnp.concatenate([p[i] for i in range(n.n_row)], axis=1) for p in (p_high, p_low)]
    for k in range(n.nodes):
        if k % CORES == 0:
            x_t = product(m_sel[k // CORES].T, *p_all)
        at = k % CORES * n.wide
        spread = jnp.concatenate([m[k : k + 1, :] for m in mask], axis=1)
        part = -x_t[at : at + n.wide, :] * spread
        own = part[:, :LANES]
        for i in range(1, n.n_row):
            own = jnp.where(r == i, part[:, i * LANES : (i + 1) * LANES], own)
        columns[pl.ds(k, n.wide, stride=n.nodes), :] = own
        wide = product(part, m_high[k], m_low[k])
        for t in range(n.tiles):
            line = pl.ds(t * n.nodes + k, n.wide, stride=n.slots)
            schur[line, :] = diag[line, :] - wide[:, t * LANES : (t + 1) * LANES]


def choose(core, pair):
    return jnp.where(core == 0, pair[0], pair[1])


def fast(n, inv_known, pattern, factor, listed, diag_inverse):
    def shape(*dims):
        return jax.ShapeDtypeStruct(dims, jnp.float32)

    def route(array, change):
        pairs = []
        for r in range(n.n_row):
            for z in range(n.n_z):
                for core in range(CORES):
                    r2, z2, core2 = change(r, z, core)
                    pairs.append(((r * n.n_z + z) * CORES + core, (r2 * n.n_z + z2) * CORES + core2))
        return lax.ppermute(array, AXES, pairs)

    def over_z(array, s):
        return route(array, lambda r, z, core: (r, z ^ s, core))

    def over_core(array):
        return route(array, lambda r, z, core: (r, z, core ^ 1))

    steps = [1 << i for i in range(n.n_row.bit_length() - 1)]

    def over_pair(array, i):
        return route(array, lambda r, z, core: (r ^ (steps[i] if core == 0 else steps[-1 - i]), z, core))

    def view(array):
        lead = array.shape[0]
        split = array.reshape(lead, n.nodes, n.tiles, LANES)
        return jnp.transpose(split, (0, 2, 1, 3)).reshape(lead * n.slots, LANES)

    taken = [pltpu.with_memory_space_constraint(a, pltpu.HBM) for a in (view(factor), listed.T, inv_known.T, pattern.T)]
    out = shape(n.bulk, LANES)
    bulk = pl.pallas_call(
        functools.partial(pack_kernel, n),
        in_specs=[pl.BlockSpec(memory_space=pltpu.HBM)] * 4,
        out_specs=VMEM,
        out_shape=out,
        scratch_shapes=[pltpu.VMEM(a.shape, a.dtype) for a in taken]
        + [pltpu.VMEM((8, LANES), jnp.float32), pltpu.SemaphoreType.DMA((len(taken),))],
        compiler_params=room(out, *taken),
    )(*taken)

    def join(*arrays):
        out = shape(sum(a.shape[0] for a in arrays), LANES)
        return pl.pallas_call(
            functools.partial(join_kernel, n),
            in_specs=[VMEM] * len(arrays),
            out_specs=VMEM,
            out_shape=out,
            compiler_params=room(out),
        )(*arrays)

    one, two = steps
    side, turn, both = (one, two), (two, one), (one ^ two, one ^ two)
    near, across = 1, n.n_z - 1
    z1, z3 = over_z(bulk, near), over_z(bulk, across)
    z2 = over_z(z1, across)
    mid, z1 = lax.optimization_barrier((bulk, z1))
    early = [bulk, over_pair(mid, 0), over_pair(mid, 1)]
    early.append(over_pair(early[1], 1))
    outer = join(z1, z3)
    trip = [over_pair(outer, 0), over_pair(outer, 1), over_pair(z2, 0), over_pair(z2, 1)]
    trip = lax.optimization_barrier(trip)
    low = n.bulk * 5 // 6 // 8 * 8
    out = [shape(n.bulk + low, LANES), shape(2 * n.bulk - low, LANES)]
    ends = pl.pallas_call(
        functools.partial(cut_kernel, n, low),
        in_specs=[VMEM] * 4,
        out_specs=[VMEM] * 2,
        out_shape=out,
        compiler_params=room(*out),
    )(*trip)
    last = join(over_pair(ends[0], 1), over_pair(ends[1], 0))
    part = [join(*early, outer, z2)]
    part.append(join(*trip))
    here = (0, 0)
    shell, beyond = (near, across), (near ^ across,)
    pieces = [(here, (0,)), (side, (0,)), (turn, (0,)), (both, (0,)), (here, shell), (here, beyond)]
    pieces = [pieces, [(side, shell), (turn, shell), (side, beyond), (turn, beyond)]]
    def short(*dims):
        return [jax.ShapeDtypeStruct(dims, jnp.bfloat16)] * 2

    store = [
        *short(n.nodes, n.total, n.width),
        shape(n.nodes // CORES, n.total, LANES),
        *short(n.n_row, n.n_col * n.rows_c, LANES),
        shape(n.n_row, n.n_col, 8, LANES),
    ]
    taken = [*part, *[over_core(p) for p in part]]
    placed = pl.pallas_call(
        functools.partial(fill_kernel, n, pieces),
        in_specs=[VMEM] * len(taken),
        out_specs=[VMEM] * len(store),
        out_shape=store,
        compiler_params=room(*taken, *store),
    )(*taken)
    pieces = [(both, (near, near ^ across, across))]
    taken = [last, over_core(last), *placed, view(diag_inverse)]
    out = [shape(n.wide * n.nodes, LANES), shape(n.wide * n.slots, LANES), *store]
    columns, schur, *_ = pl.pallas_call(
        functools.partial(work_kernel, n, pieces),
        in_specs=[VMEM] * len(taken),
        out_specs=[VMEM] * len(out),
        out_shape=out,
        input_output_aliases={2 + i: 2 + i for i in range(len(store))},
        compiler_params=room(*taken, *out),
    )(*taken)
    schur = jnp.transpose(schur.reshape(n.wide, n.tiles, n.nodes, LANES), (0, 2, 1, 3))
    return columns.reshape(n.wide, n.nodes, LANES), schur.reshape(n.wide, n.nodes, n.width)


def local(inv_known, pattern, factor, listed, diag_inverse):
    n = Sizes(inv_known, pattern, factor, diag_inverse)
    plan = functools.partial(fast, n) if n.fits() else general
    return plan(inv_known, pattern, factor, listed, diag_inverse)


def solution(mesh):
    in_specs = (
        P("row", "col"),
        P("row", "col"),
        P(("row", "col"), None, None),
        P(("row", "col"), None),
        P("col", None, None),
    )
    out_specs = (P("col", None, "row"), P("col", None, None))
    return jax.shard_map(local, mesh=mesh, in_specs=in_specs, out_specs=out_specs, check_vma=False)
```
